32 devices in a mesh: section: 2 (over x), expert: 16 (over z, y, core).
Axes of the slice: x: 2, y: 2, z: 4, core: 2. Of those that a mesh axis runs over, the one named last changes fastest.
Arguments:
- forward_tokens: bfloat16 [2, 1024, 2048], P('section', 'expert'), may hold values from -6 to 6
- forward_choice: int32 [2, 1024, 8], P('section', 'expert'), may hold values from 0 to 15, all different within a row; in each aligned block of 64 rows (0 to 63, 64 to 127, ..., all dimensions but the last counted through in order) at most 36 rows name the same one
- forward_gates: float32 [2, 1024, 8], P('section', 'expert'), may hold values from 0.1 to 1
- backward_tokens: bfloat16 [2, 1024, 2048], P('section', 'expert'), may hold values from -6 to 6
- backward_cotangent: bfloat16 [2, 1024, 2048], P('section', 'expert'), may hold values from -6 to 6
- backward_choice: int32 [2, 1024, 8], P('section', 'expert'), may hold values from 0 to 15, all different within a row; in each aligned block of 64 rows (0 to 63, 64 to 127, ..., all dimensions but the last counted through in order) at most 36 rows name the same one
- backward_gates: float32 [2, 1024, 8], P('section', 'expert'), may hold values from 0.1 to 1
- norm_gain: float32 [2, 2048], P('section'), may hold values from 0.1 to 1.9
- gate_weight: bfloat16 [2, 16, 2048, 768], P('section', 'expert'), may hold values from -0.125 to 0.125
- up_weight: bfloat16 [2, 16, 2048, 768], P('section', 'expert'), may hold values from -0.125 to 0.125
- down_weight: bfloat16 [2, 16, 768, 2048], P('section', 'expert'), may hold values from -0.21875 to 0.21875
Outputs:
- section_input: bfloat16 [2, 1024, 2048], P('section', 'expert')
- section_gradient: bfloat16 [2, 1024, 2048], P('section', 'expert')
The draws below stay inside these ranges and needn't reach their ends.
Inputs may be any that keep to these rules, and one draw needn't show every extreme that they name: `forward_choice`: each token names 8 different experts; among the tokens of one device no expert is named more than 36 times, and in every draw some expert of some device is named exactly 36 times. `backward_choice`: each token names 8 different experts; among the tokens of one device no expert is named more than 36 times, and in every draw some expert of some device is named exactly 36 times.
All inputs are finite; a program needn't handle non-finite values.
Results may differ from the reference program's by a relative error of at most 0.0069.
Values may be sent and summed in bfloat16 or wider, within the bound.
No kernel may reach another device: no remote copies, remote signals or barrier semaphores. Data moves between devices by JAX's collectives and lax.ppermute only.
A program may use at most 128 MiB of HBM per device.

```python
import math
import jax
import jax.numpy as jnp
import numpy as np
from jax import lax

D = 2048
FF = 768
TOPK = 8
TOK_DEV = 64
EXPERTS = 16
CAP = 36
TOKENS = 1024
SECTIONS = 2
N_EXPERT = 16


def block_scale(rng, extent, split, low, top_value):
    loudness = 1.0
    for position, blocks in split:
        steps = jax.random.uniform(jax.random.fold_in(jax.random.fold_in(rng, 6), position), (blocks,), jnp.float32, low / len(split), top_value / len(split))
        loudness = loudness * jnp.repeat(jnp.exp(steps), extent[position] // blocks).reshape((-1,) + (1,) * (len(extent) - 1 - position))
    return loudness


def deal_out(stream_key, own, number, rows, number_of, top, most, lean):
    order = jax.random.permutation(stream_key, number_of)
    heavy_load, usual = portions_of(number_of, rows * top, most, lean, True), portions_of(number_of, rows * top, most, lean, False)
    places = jnp.arange(number_of)

    def named(tallies, turn):
        used = int((tallies > 0).sum())
        fixed = max(1, used // 4)
        shifted = fixed + (places - fixed + turn * (used - fixed)) % max(1, number_of - fixed)
        return jnp.zeros((number_of,), jnp.int32).at[order[jnp.where(places < fixed, places, shifted)]].set(jnp.asarray(tallies, jnp.int32))

    tallies = jnp.where(number % 4 == 0, named(heavy_load, number // 4), named(usual, number - number // 4 - 1))
    mixed = jax.random.permutation(jax.random.fold_in(own, 3), number_of)
    giver, taker = mixed[0:number_of // 2 * 2:2], mixed[1:number_of // 2 * 2:2]
    slack = jnp.minimum(tallies[giver] - 1, most - tallies[taker]) // 2
    slack = jnp.where((giver == order[0]) | (taker == order[0]) | (tallies[taker] == 0), 0, jnp.maximum(slack, 0))
    shifted = jax.random.randint(jax.random.fold_in(own, 4), (number_of // 2,), 0, 1 << 20) % (slack + 1)
    tallies = tallies.at[giver].add(-shifted).at[taker].add(shifted)
    items = jnp.searchsorted(jnp.cumsum(tallies), jnp.arange(rows * top), side="right").astype(jnp.int32)
    listing = items.reshape(top, rows).T
    listing = listing[jax.random.permutation(jax.random.fold_in(own, 1), rows)]
    turn = jax.random.randint(jax.random.fold_in(own, 2), (rows, 1), 0, top)
    return jnp.take_along_axis(listing, (jnp.arange(top)[None, :] + turn) % top, axis=1)


def portions_of(amount, total, reach, lean, full):
    portions = [(1 << 20) // math.isqrt(standing ** lean) + 1 for standing in range(1, amount + 1)]
    largest = reach if full else min(reach, max(-(-total // amount), total * portions[0] // sum(portions)))
    least = 1 if total - largest >= amount - 1 else 0
    counts, spare = [largest] + [least] * (amount - 1), total - largest - least * (amount - 1)
    while spare > 0:
        movable = [i for i in range(1, amount) if counts[i] < largest] or [i for i in range(1, amount) if counts[i] < reach]
        whole, budget = sum([portions[i] for i in movable]), spare
        for i in movable:
            more = min(reach - counts[i], max(1, budget * portions[i] // whole), spare)
            counts[i] = counts[i] + more
            spare = spare - more
    return np.array(counts)


def scatter_about(stream_key, dims, deviation, bound, pieces=(), kind=jnp.bfloat16):
    level = block_scale(stream_key, dims, pieces, -0.22, 0.18) if pieces else 1.0
    array = jax.random.normal(stream_key, dims, jnp.float32) * deviation * level
    return jnp.minimum(jnp.maximum(array, -bound), bound).astype(kind)


def setup_inputs(seed: int = 0) -> dict:
    streams_of = jax.random.split(jax.random.key(seed), 12)
    forward_tokens = scatter_about(streams_of[0], (SECTIONS, TOKENS, D), 1.0, 6.0, ((0, 2), (1, 16)))
    forward_choice_keys = jax.random.split(jax.random.fold_in(streams_of[1], 1), SECTIONS * TOKENS // TOK_DEV)
    forward_choice_turns = jax.random.permutation(jax.random.fold_in(streams_of[1], 3), SECTIONS * TOKENS // TOK_DEV)
    forward_choice = jax.vmap(lambda own, number: deal_out(jax.random.fold_in(streams_of[1], 2), own, number, TOK_DEV, EXPERTS, TOPK, CAP, 2))(forward_choice_keys, forward_choice_turns).reshape((SECTIONS, TOKENS, TOPK))
    forward_gates = jnp.clip(jnp.exp(math.log(1.0) - 2.3025851 * jax.random.uniform(streams_of[2], (SECTIONS, TOKENS, TOPK), jnp.float32) ** block_scale(streams_of[2], (SECTIONS, TOKENS, TOPK), ((0, 2), (1, 16)), -0.2, 0.2)), 0.1, 1.0)
    backward_tokens = scatter_about(streams_of[3], (SECTIONS, TOKENS, D), 1.0, 6.0, ((0, 2), (1, 16)))
    backward_cotangent = scatter_about(streams_of[4], (SECTIONS, TOKENS, D), 1.0, 6.0, ((0, 2), (1, 16)))
    backward_choice_keys = jax.random.split(jax.random.fold_in(streams_of[5], 1), SECTIONS * TOKENS // TOK_DEV)
    backward_choice_turns = jax.random.permutation(jax.random.fold_in(streams_of[5], 3), SECTIONS * TOKENS // TOK_DEV)
    backward_choice = jax.vmap(lambda own, number: deal_out(jax.random.fold_in(streams_of[5], 2), own, number, TOK_DEV, EXPERTS, TOPK, CAP, 2))(backward_choice_keys, backward_choice_turns).reshape((SECTIONS, TOKENS, TOPK))
    backward_gates = jnp.clip(jnp.exp(math.log(1.0) - 2.3025851 * jax.random.uniform(streams_of[6], (SECTIONS, TOKENS, TOPK), jnp.float32) ** block_scale(streams_of[6], (SECTIONS, TOKENS, TOPK), ((0, 2), (1, 16)), -0.2, 0.2)), 0.1, 1.0)
    norm_gain = jnp.clip(1.0 + 0.18 * jax.random.normal(streams_of[7], (SECTIONS, D), jnp.float32), 0.1, 1.9)
    gate_weight = scatter_about(streams_of[8], (SECTIONS, EXPERTS, D, FF), D ** -0.5, 0.125, ((0, 2), (1, 16)))
    up_weight = scatter_about(streams_of[9], (SECTIONS, EXPERTS, D, FF), D ** -0.5, 0.125, ((0, 2), (1, 16)))
    down_weight = scatter_about(streams_of[10], (SECTIONS, EXPERTS, FF, D), FF ** -0.5, 0.21875, ((0, 2), (1, 16)))
    return {"forward_tokens": forward_tokens, "forward_choice": forward_choice, "forward_gates": forward_gates, "backward_tokens": backward_tokens, "backward_cotangent": backward_cotangent, "backward_choice": backward_choice, "backward_gates": backward_gates, "norm_gain": norm_gain, "gate_weight": gate_weight, "up_weight": up_weight, "down_weight": down_weight}


norm_epsilon = 1e-06

def slot_ranks(choices_flat):
    length = choices_flat.shape[0]
    same_expert = choices_flat[:, None] == choices_flat[None, :]
    earlier = lax.broadcasted_iota(jnp.int32, (length, length), 1) < lax.broadcasted_iota(jnp.int32, (length, length), 0)
    return lax.optimization_barrier(jnp.sum((same_expert & earlier).astype(jnp.int32), axis=1)).astype(jnp.int32)

def normalize(tokens, gain_row):
    tokens_f32 = tokens.astype(jnp.float32)
    inverse = lax.rsqrt(lax.optimization_barrier(jnp.mean(tokens_f32 * tokens_f32, axis=-1, keepdims=True)) + norm_epsilon)
    normed = (tokens_f32 * inverse * gain_row).astype(jnp.bfloat16)
    return (tokens_f32, inverse, normed)

def dot_plain(left, right):
    return jnp.dot(left, right, preferred_element_type=jnp.float32)

def dot_trans(left, right):
    return lax.dot_general(left, right, (((1,), (1,)), ((), ())), preferred_element_type=jnp.float32)

def expert_forward(normed, gate_w, up_w, down_w):
    gate_act = dot_plain(normed, gate_w)
    up_act = dot_plain(normed, up_w)
    hidden = (jax.nn.silu(gate_act) * up_act).astype(jnp.bfloat16)
    return dot_plain(hidden, down_w).astype(jnp.bfloat16)

def expert_backward(normed, out_grad, gate_w, up_w, down_w):
    gate_act = dot_plain(normed, gate_w)
    up_act = dot_plain(normed, up_w)
    hidden_grad = dot_trans(out_grad, down_w)
    sigmoid_val = jax.nn.sigmoid(gate_act)
    silu_val = gate_act * sigmoid_val
    silu_slope = sigmoid_val * (1.0 + gate_act * (1.0 - sigmoid_val))
    gate_grad = (hidden_grad * up_act * silu_slope).astype(jnp.bfloat16)
    up_grad = (hidden_grad * silu_val).astype(jnp.bfloat16)
    return (dot_trans(gate_grad, gate_w) + dot_trans(up_grad, up_w)).astype(jnp.bfloat16)

def global_slots(expert_ids):
    blocks = expert_ids.reshape(N_EXPERT, TOK_DEV * TOPK)
    ranks_all = jax.vmap(slot_ranks)(blocks).reshape(TOKENS, TOPK)
    source = (jnp.arange(TOKENS, dtype=jnp.int32) // TOK_DEV).astype(jnp.int32)
    return ((expert_ids * N_EXPERT + source[:, None]) * CAP + ranks_all).reshape(-1).astype(jnp.int32)

def fill_buffer(per_slot, slot_flat):
    buffer = jnp.zeros((EXPERTS * N_EXPERT * CAP, D), jnp.bfloat16).at[slot_flat].set(per_slot)
    return buffer.reshape(EXPERTS, N_EXPERT * CAP, D)

def one_section(fwd_rows, fwd_ids, fwd_gates, back_rows, cotangent, back_ids, back_gates, gain_row, gate_w, up_w, down_w):
    _, _, fwd_normed = normalize(fwd_rows, gain_row)
    fwd_slots = global_slots(fwd_ids)
    fwd_buffer = fill_buffer(jnp.repeat(fwd_normed, TOPK, axis=0), fwd_slots)

    def run_forward(operands):
        return expert_forward(operands[0], operands[1], operands[2], operands[3])
    fwd_out = lax.map(run_forward, (fwd_buffer, gate_w, up_w, down_w)).reshape(-1, D)
    picked = fwd_out[fwd_slots].reshape(TOKENS, TOPK, D).astype(jnp.float32)
    mixed_out = fwd_rows.astype(jnp.float32) + lax.optimization_barrier(jnp.sum(fwd_gates[:, :, None] * picked, axis=1))
    back_f32, back_inverse, back_normed = normalize(back_rows, gain_row)
    back_slots = global_slots(back_ids)
    back_buffer = fill_buffer(jnp.repeat(back_normed, TOPK, axis=0), back_slots)
    cot_f32 = cotangent.astype(jnp.float32)
    slot_grads = (back_gates[:, :, None] * cot_f32[:, None, :]).astype(jnp.bfloat16).reshape(-1, D)
    grad_buffer = fill_buffer(slot_grads, back_slots)

    def run_backward(operands):
        return expert_backward(operands[0], operands[1], operands[2], operands[3], operands[4])
    back_out = lax.map(run_backward, (back_buffer, grad_buffer, gate_w, up_w, down_w)).reshape(-1, D)
    grad_sum = lax.optimization_barrier(jnp.sum(back_out[back_slots].reshape(TOKENS, TOPK, D).astype(jnp.float32), axis=1))
    scaled = gain_row * grad_sum
    mean_term = lax.optimization_barrier(jnp.mean(back_f32 * scaled, axis=-1, keepdims=True))
    token_grad = cot_f32 + back_inverse * scaled - back_f32 * back_inverse * back_inverse * back_inverse * mean_term
    return (mixed_out.astype(jnp.bfloat16), token_grad.astype(jnp.bfloat16))

def reference(forward_tokens, forward_choice, forward_gates, backward_tokens, backward_cotangent, backward_choice, backward_gates, norm_gain, gate_weight, up_weight, down_weight):
    mixed_list = []
    grad_list = []
    for section_index in range(SECTIONS):
        mixed_out, token_grad = one_section(forward_tokens[section_index], forward_choice[section_index], forward_gates[section_index], backward_tokens[section_index], backward_cotangent[section_index], backward_choice[section_index], backward_gates[section_index], norm_gain[section_index], gate_weight[section_index], up_weight[section_index], down_weight[section_index])
        mixed_list.append(mixed_out)
        grad_list.append(token_grad)
    section_input = jnp.roll(jnp.stack(mixed_list), 1, axis=0)
    section_gradient = jnp.roll(jnp.stack(grad_list), -1, axis=0)
    return (section_input, section_gradient)
```

```python
import jax
import jax.numpy as jnp
from jax import lax
from jax.sharding import PartitionSpec as P

norm_epsilon = 1e-06
CORES = 2
META = 128


def ring_order(chips):
    return [*range(0, chips, 2), *reversed(range(1, chips, 2))]


def ring_route(devices, distance):
    order = ring_order(devices // CORES)
    chips = len(order)
    return [
        (chip * CORES + core, order[(place + distance) % chips] * CORES + core)
        for place, chip in enumerate(order)
        for core in range(CORES)
    ]


def core_route(devices):
    return [(i, i ^ 1) for i in range(devices)]


def passed_along(block, axis, distance):
    size = lax.axis_size(axis)
    return lax.ppermute(block, axis, [(i, (i + distance) % size) for i in range(size)])


def ring_gather(block):
    devices = lax.axis_size("expert")
    reach = devices // CORES // 2
    up, down = ring_route(devices, 1), ring_route(devices, -1)
    half = block.shape[0] // 2
    gathered, behind, ahead = [block], block, block
    for _ in range(reach - 1):
        behind = lax.ppermute(behind, "expert", up)
        ahead = lax.ppermute(ahead, "expert", down)
        gathered += [behind, ahead]
    low = lax.ppermute(behind[:half], "expert", up)
    high = lax.ppermute(ahead[half:], "expert", down)
    return gathered + [low, high]


def ring_scatter(parts):
    devices = lax.axis_size("expert")
    reach = devices // CORES // 2
    up, down = ring_route(devices, 1), ring_route(devices, -1)
    half = parts[0].shape[0] // 2
    low, high = parts[-2], parts[-1]
    behind = lax.ppermute(low.astype(jnp.bfloat16), "expert", down)
    ahead = lax.ppermute(high.astype(jnp.bfloat16), "expert", up)
    for distance in range(reach - 1, 0, -1):
        to_behind, to_ahead = parts[2 * distance - 1], parts[2 * distance]
        if distance == reach - 1:
            behind = jnp.concatenate(
                [to_behind[:half] + behind.astype(jnp.float32), to_behind[half:]]
            )
            ahead = jnp.concatenate(
                [to_ahead[:half], to_ahead[half:] + ahead.astype(jnp.float32)]
            )
        else:
            behind = to_behind + behind.astype(jnp.float32)
            ahead = to_ahead + ahead.astype(jnp.float32)
        behind = lax.ppermute(behind.astype(jnp.bfloat16), "expert", down)
        ahead = lax.ppermute(ahead.astype(jnp.bfloat16), "expert", up)
    return parts[0] + behind.astype(jnp.float32) + ahead.astype(jnp.float32)


def split_rows(array, rows):
    blocks = array.shape[0] // rows
    half = rows // 2
    parts = [array[i * rows : (i + 1) * rows] for i in range(blocks - 1)]
    last = array[(blocks - 1) * rows :]
    return parts + [last[:half], last[half:]]


def normalize(tokens, gain_row):
    tokens_f32 = tokens.astype(jnp.float32)
    inverse = lax.rsqrt(jnp.mean(tokens_f32 * tokens_f32, axis=-1, keepdims=True) + norm_epsilon)
    normed = (tokens_f32 * inverse * gain_row).astype(jnp.bfloat16)
    return (tokens_f32, inverse, normed)


def routing_columns(choice, gates):
    high = gates.astype(jnp.bfloat16)
    low = (gates - high.astype(jnp.float32)).astype(jnp.bfloat16)
    return [choice.astype(jnp.bfloat16), high, low]


def gate_of(columns, expert):
    top = columns.shape[1] // 3
    columns = columns.astype(jnp.float32)
    choice, gates = columns[:, :top], columns[:, top : 2 * top] + columns[:, 2 * top :]
    return jnp.sum(
        jnp.where(choice == expert.astype(jnp.float32), gates, 0.0), axis=1, keepdims=True
    )


def dot_plain(left, right):
    return jnp.dot(left, right, preferred_element_type=jnp.float32)


def dot_trans(left, right):
    return lax.dot_general(
        left, right, (((1,), (1,)), ((), ())), preferred_element_type=jnp.float32
    )


def expert_forward(normed, gate, gate_w, up_w, down_w):
    gate_act = dot_plain(normed, gate_w)
    up_act = dot_plain(normed, up_w)
    hidden = (jax.nn.silu(gate_act) * up_act * gate).astype(jnp.bfloat16)
    return dot_plain(hidden, down_w)


def expert_backward(normed, cotangent, gate, gate_w, up_w, down_w):
    gate_act = dot_plain(normed, gate_w)
    up_act = dot_plain(normed, up_w)
    hidden_grad = dot_trans(cotangent, down_w) * gate
    sigmoid_val = jax.nn.sigmoid(gate_act)
    silu_val = gate_act * sigmoid_val
    silu_slope = sigmoid_val * (1.0 + gate_act * (1.0 - sigmoid_val))
    gate_grad = (hidden_grad * up_act * silu_slope).astype(jnp.bfloat16)
    up_grad = (hidden_grad * silu_val).astype(jnp.bfloat16)
    return dot_trans(gate_grad, gate_w) + dot_trans(up_grad, up_w)


def per_device(
    forward_tokens,
    forward_choice,
    forward_gates,
    backward_tokens,
    backward_cotangent,
    backward_choice,
    backward_gates,
    norm_gain,
    gate_weight,
    up_weight,
    down_weight,
):
    tok_count, width = forward_tokens.shape[1:]
    top = forward_choice.shape[2]
    gain_row = norm_gain[0]
    swap = core_route(lax.axis_size("expert"))
    mine = (gate_weight[0, 0], up_weight[0, 0], down_weight[0, 0])
    theirs = tuple(lax.ppermute(w, "expert", swap) for w in mine)
    me = lax.axis_index("expert")
    sibling = me + 1 - 2 * lax.rem(me, 2)

    forward_rows = forward_tokens[0]
    _, _, fwd_normed = normalize(forward_rows, gain_row)
    back_f32, back_inverse, back_normed = normalize(backward_tokens[0], gain_row)
    columns = routing_columns(forward_choice[0], forward_gates[0]) + routing_columns(
        backward_choice[0], backward_gates[0]
    )
    used = 6 * top
    pad = -used % META
    columns.append(jnp.zeros((tok_count, pad), jnp.bfloat16))
    fwd_blocks = ring_gather(jnp.concatenate([fwd_normed] + columns, axis=1))
    back_blocks = ring_gather(jnp.concatenate([back_normed, backward_cotangent[0]], axis=1))

    fwd_all = jnp.concatenate(fwd_blocks)
    fwd_x = fwd_all[:, :width]
    fwd_columns = fwd_all[:, width : width + 3 * top]
    back_columns = fwd_all[:, width + 3 * top : width + used]
    out = expert_forward(fwd_x, gate_of(fwd_columns, me), *mine) + expert_forward(
        fwd_x, gate_of(fwd_columns, sibling), *theirs
    )
    mixed_out = forward_rows.astype(jnp.float32) + ring_scatter(split_rows(out, tok_count))

    back_all = jnp.concatenate(back_blocks)
    back_x, back_cot = back_all[:, :width], back_all[:, width:]
    out = expert_backward(back_x, back_cot, gate_of(back_columns, me), *mine) + expert_backward(
        back_x, back_cot, gate_of(back_columns, sibling), *theirs
    )
    grad_sum = ring_scatter(split_rows(out, tok_count))
    scaled = gain_row * grad_sum
    mean_term = jnp.mean(back_f32 * scaled, axis=-1, keepdims=True)
    token_grad = (
        backward_cotangent[0].astype(jnp.float32)
        + back_inverse * scaled
        - back_f32 * back_inverse * back_inverse * back_inverse * mean_term
    )
    section_input = passed_along(mixed_out.astype(jnp.bfloat16)[None], "section", 1)
    section_gradient = passed_along(token_grad.astype(jnp.bfloat16)[None], "section", -1)
    return (section_input, section_gradient)


def solution(mesh):
    rows = P("section", "expert", None)
    weights = P("section", "expert", None, None)
    return jax.shard_map(
        per_device,
        mesh=mesh,
        in_specs=(rows,) * 7 + (P("section", None),) + (weights,) * 3,
        out_specs=(rows, rows),
        check_vma=False,
    )
```

```python
import functools

import jax
import jax.numpy as jnp
from jax import lax
from jax.experimental import pallas as pl
from jax.experimental.pallas import tpu as pltpu
from jax.sharding import PartitionSpec as P

norm_epsilon = 1e-06
CORES = 2
LANES = 128
TILE = 256
ROWS_AT_ONCE = 256
MIB = 1 << 20
IN_HBM = pl.BlockSpec(memory_space=pl.ANY)
IN_VMEM = pl.BlockSpec(memory_space=pltpu.VMEM)
IN_SMEM = pl.BlockSpec(memory_space=pltpu.SMEM)


def ring_order(chips):
    return [*range(0, chips, 2), *reversed(range(1, chips, 2))]


def ring_route(devices, distance):
    order = ring_order(devices // CORES)
    chips = len(order)
    return [
        (chip * CORES + core, order[(place + distance) % chips] * CORES + core)
        for place, chip in enumerate(order)
        for core in range(CORES)
    ]


def core_route(devices):
    return [(i, i ^ 1) for i in range(devices)]


def passed_along(block, axis, distance):
    size = lax.axis_size(axis)
    return lax.ppermute(block, axis, [(i, (i + distance) % size) for i in range(size)])


def after(arrays, others):
    count = len(arrays)
    return lax.optimization_barrier((*arrays, *others))[:count]


class RingGather:
    def __init__(self, block):
        self.blocks = [block]
        self.newest = (block, block)
        self.left = lax.axis_size("expert") // CORES // 2

    def step(self, others=()):
        devices = lax.axis_size("expert")
        behind, ahead = after(self.newest, others)
        self.left -= 1
        if not self.left:
            half = behind.shape[0] // 2
            behind, ahead = behind[:half], ahead[half:]
        behind = lax.ppermute(behind, "expert", ring_route(devices, 1))
        ahead = lax.ppermute(ahead, "expert", ring_route(devices, -1))
        self.newest = (behind, ahead)
        self.blocks += self.newest


class RingScatter:
    def __init__(self, parts):
        self.parts = parts
        self.newest = ()
        self.reach = self.left = lax.axis_size("expert") // CORES // 2

    def step(self, others=()):
        devices = lax.axis_size("expert")
        to_behind, to_ahead = self.parts[2 * self.left - 1], self.parts[2 * self.left]
        if self.left == self.reach:
            behind, ahead = to_behind, to_ahead
        else:
            behind, ahead = after(self.newest, others)
            half = self.parts[0].shape[0] // 2
            if self.left == self.reach - 1:
                behind = jnp.concatenate([added(to_behind[:half], behind), to_behind[half:]])
                ahead = jnp.concatenate([to_ahead[:half], added(to_ahead[half:], ahead)])
            else:
                behind, ahead = added(to_behind, behind), added(to_ahead, ahead)
        self.left -= 1
        behind = lax.ppermute(behind, "expert", ring_route(devices, -1))
        ahead = lax.ppermute(ahead, "expert", ring_route(devices, 1))
        self.newest = (behind, ahead)

    def total(self):
        behind, ahead = self.newest
        return self.parts[0].astype(jnp.float32) + behind.astype(jnp.float32) + ahead.astype(jnp.float32)


def added(left, right):
    return (left.astype(jnp.float32) + right.astype(jnp.float32)).astype(jnp.bfloat16)


def inverse_norm(rows):
    return lax.rsqrt(jnp.mean(rows * rows, axis=-1, keepdims=True) + norm_epsilon)


def normalize(tokens, gain_row):
    tokens_f32 = tokens.astype(jnp.float32)
    return (tokens_f32 * inverse_norm(tokens_f32) * gain_row).astype(jnp.bfloat16)


def gate_table(choice, gates, experts):
    named = choice[:, :, None] == jnp.arange(experts)
    table = jnp.sum(jnp.where(named, gates[:, :, None], 0.0), axis=1)
    high = table.astype(jnp.bfloat16)
    return [high, (table - high.astype(jnp.float32)).astype(jnp.bfloat16)]


def dot_plain(left, right):
    return jnp.dot(left, right, preferred_element_type=jnp.float32)


def dot_trans(left, right):
    return lax.dot_general(
        left, right, (((1,), (1,)), ((), ())), preferred_element_type=jnp.float32
    )


def weights_body(*refs):
    weights, (gate_up, down, done) = refs[:6], refs[6:]
    hidden = weights[0].shape[1]
    copies = []
    for core in range(CORES):
        gate_w, up_w, down_w = weights[3 * core : 3 * core + 3]
        first = gate_up.at[:, pl.ds(2 * core * hidden, hidden)]
        second = gate_up.at[:, pl.ds((2 * core + 1) * hidden, hidden)]
        copies += [(gate_w, first), (up_w, second), (down_w, down.at[pl.ds(core * hidden, hidden)])]
    copies = [pltpu.make_async_copy(*pair, done.at[i]) for i, pair in enumerate(copies)]
    for copy in copies:
        copy.start()
    for copy in copies:
        copy.wait()


def weights_in_vmem(mine, theirs):
    width, hidden = mine[0].shape
    return pl.pallas_call(
        weights_body,
        in_specs=[IN_HBM] * 6,
        out_specs=(IN_VMEM, IN_VMEM),
        out_shape=(
            pltpu.VMEM((width, 2 * CORES * hidden), jnp.bfloat16),
            pltpu.VMEM((CORES * hidden, width), jnp.bfloat16),
        ),
        scratch_shapes=[pltpu.SemaphoreType.DMA((6,))],
        compiler_params=pltpu.CompilerParams(vmem_limit_bytes=24 * MIB),
    )(*mine, *theirs)


def collect(blocks, rows, arrived):
    copies, first = [], 0
    for i, block in enumerate(blocks):
        to = rows.at[pl.ds(first, block.shape[0])]
        copies.append(pltpu.make_async_copy(block, to, arrived.at[i]))
        first += block.shape[0]
    for copy in copies:
        copy.start()
    for copy in copies:
        copy.wait()


def backward_body(count, devices, *refs):
    blocks = refs[:count]
    experts, gate_up, down, out, forward_gates, rows, grads, arrived = refs[count:]
    width, hidden = gate_up.shape[0], down.shape[0] // CORES
    collect(blocks, rows, arrived)
    table = rows[:, 2 * width :].astype(jnp.float32)
    lane = lax.broadcasted_iota(jnp.int32, table.shape, 1)

    def gate(first, core):
        ours = first * devices + experts[core]
        named = (lane == ours) | (lane == ours + devices)
        return jnp.sum(jnp.where(named, table, 0.0), axis=1, keepdims=True)

    out_lane = lax.broadcasted_iota(jnp.int32, forward_gates.shape, 1)
    forward_gates[...] = jnp.where(out_lane == 0, gate(0, 0), gate(0, 1))
    for core in range(CORES):
        scale = gate(2, core)
        for tile in range(0, hidden, TILE):
            gate_at = pl.ds(2 * core * hidden + tile, TILE)
            up_at = pl.ds((2 * core + 1) * hidden + tile, TILE)
            down_at = pl.ds(core * hidden + tile, TILE)
            gate_act = dot_plain(rows[:, :width], gate_up[:, gate_at])
            up_act = dot_plain(rows[:, :width], gate_up[:, up_at])
            hidden_grad = dot_trans(rows[:, width : 2 * width], down[down_at, :]) * scale
            sigmoid_val = jax.nn.sigmoid(gate_act)
            silu_slope = sigmoid_val * (1.0 + gate_act * (1.0 - sigmoid_val))
            grads[:, gate_at] = (hidden_grad * up_act * silu_slope).astype(jnp.bfloat16)
            grads[:, up_at] = (hidden_grad * (gate_act * sigmoid_val)).astype(jnp.bfloat16)
    for tile in range(0, width, TILE):
        at = pl.ds(tile, TILE)
        out[:, at] = dot_trans(grads[...], gate_up[at, :]).astype(jnp.bfloat16)


def experts_backward(blocks, experts, gate_up, down, devices):
    count, rows = sum(b.shape[0] for b in blocks), blocks[0].shape[1]
    width = gate_up.shape[0]
    return pl.pallas_call(
        functools.partial(backward_body, len(blocks), devices),
        in_specs=[IN_HBM] * len(blocks) + [IN_SMEM, IN_VMEM, IN_VMEM],
        out_specs=(IN_VMEM, IN_VMEM),
        out_shape=(
            jax.ShapeDtypeStruct((count, width), jnp.bfloat16),
            jax.ShapeDtypeStruct((count, LANES), jnp.float32),
        ),
        scratch_shapes=[
            pltpu.VMEM((count, rows), jnp.bfloat16),
            pltpu.VMEM((count, gate_up.shape[1]), jnp.bfloat16),
            pltpu.SemaphoreType.DMA((len(blocks),)),
        ],
        compiler_params=pltpu.CompilerParams(vmem_limit_bytes=20 * MIB),
        cost_estimate=pl.CostEstimate(
            flops=2 * count * width * down.shape[0] * 5,
            bytes_accessed=count * (rows + width) * 2,
            transcendentals=0,
        ),
    )(*blocks, experts, gate_up, down)


def forward_body(count, *refs):
    blocks = refs[:count]
    gates, gate_up, down, out, rows, acts, arrived = refs[count:]
    width, hidden = gate_up.shape[0], down.shape[0] // CORES
    collect(blocks, rows, arrived)
    for core in range(CORES):
        scale = gates[:, core : core + 1]
        for tile in range(0, hidden, TILE):
            gate_at = pl.ds(2 * core * hidden + tile, TILE)
            up_at = pl.ds((2 * core + 1) * hidden + tile, TILE)
            gate_act = dot_plain(rows[...], gate_up[:, gate_at])
            up_act = dot_plain(rows[...], gate_up[:, up_at])
            act = gate_act * jax.nn.sigmoid(gate_act) * up_act * scale
            acts[:, pl.ds(core * hidden + tile, TILE)] = act.astype(jnp.bfloat16)
    for tile in range(0, width, TILE):
        at = pl.ds(tile, TILE)
        out[:, at] = dot_plain(acts[...], down[:, at]).astype(jnp.bfloat16)


def experts_forward(blocks, gates, gate_up, down):
    count, width = sum(b.shape[0] for b in blocks), gate_up.shape[0]
    return pl.pallas_call(
        functools.partial(forward_body, len(blocks)),
        in_specs=[IN_HBM] * len(blocks) + [IN_VMEM, IN_VMEM, IN_VMEM],
        out_specs=IN_VMEM,
        out_shape=jax.ShapeDtypeStruct((count, width), jnp.bfloat16),
        scratch_shapes=[
            pltpu.VMEM((count, width), jnp.bfloat16),
            pltpu.VMEM((count, down.shape[0]), jnp.bfloat16),
            pltpu.SemaphoreType.DMA((len(blocks),)),
        ],
        compiler_params=pltpu.CompilerParams(vmem_limit_bytes=20 * MIB),
        cost_estimate=pl.CostEstimate(
            flops=2 * count * width * down.shape[0] * 3,
            bytes_accessed=count * 2 * width * 2,
            transcendentals=0,
        ),
    )(*blocks, gates, gate_up, down)


def grouped(blocks):
    groups, rows = [[]], 0
    for block in blocks:
        if groups[-1] and rows + block.shape[0] > ROWS_AT_ONCE:
            groups.append([])
            rows = 0
        groups[-1].append(block)
        rows += block.shape[0]
    return groups


def ungrouped(outs, groups):
    parts = []
    for out, group in zip(outs, groups):
        first = 0
        for block in group:
            parts.append(out[first : first + block.shape[0]])
            first += block.shape[0]
    return parts


def per_device(
    forward_tokens,
    forward_choice,
    forward_gates,
    backward_tokens,
    backward_cotangent,
    backward_choice,
    backward_gates,
    norm_gain,
    gate_weight,
    up_weight,
    down_weight,
):
    devices = lax.axis_size("expert")
    gain_row = norm_gain[0]
    cotangent = backward_cotangent[0]
    tables = gate_table(forward_choice[0], forward_gates[0], devices) + gate_table(
        backward_choice[0], backward_gates[0], devices
    )
    pad = jnp.zeros((cotangent.shape[0], -4 * devices % LANES), jnp.bfloat16)
    back = RingGather(
        jnp.concatenate([normalize(backward_tokens[0], gain_row), cotangent, *tables, pad], axis=1)
    )
    fwd = RingGather(normalize(forward_tokens[0], gain_row))
    back.step()
    fwd.step()
    while back.left:
        arrived = back.newest
        back.step(fwd.newest)
        fwd.step(arrived)

    mine = (gate_weight[0, 0], up_weight[0, 0], down_weight[0, 0])
    theirs = tuple(lax.ppermute(w, "expert", core_route(devices)) for w in mine)
    gate_up, down = weights_in_vmem(mine, theirs)
    me = lax.axis_index("expert").astype(jnp.int32)
    experts = jnp.stack([me, me + 1 - 2 * lax.rem(me, 2)])

    back_groups, fwd_groups = grouped(back.blocks), grouped(fwd.blocks)
    back_outs = [experts_backward(g, experts, gate_up, down, devices) for g in back_groups]
    back_sum = RingScatter(ungrouped([out for out, _ in back_outs], back_groups))
    fwd_outs = [
        experts_forward(g, gates, gate_up, down) for g, (_, gates) in zip(fwd_groups, back_outs)
    ]
    fwd_sum = RingScatter(ungrouped(fwd_outs, fwd_groups))
    back_sum.step()
    fwd_sum.step()
    while back_sum.left:
        arrived = back_sum.newest
        back_sum.step(fwd_sum.newest)
        fwd_sum.step(arrived)

    back_f32 = backward_tokens[0].astype(jnp.float32)
    back_inverse = inverse_norm(back_f32)
    scaled = gain_row * back_sum.total()
    mean_term = jnp.mean(back_f32 * scaled, axis=-1, keepdims=True)
    token_grad = (
        cotangent.astype(jnp.float32)
        + back_inverse * scaled
        - back_f32 * back_inverse * back_inverse * back_inverse * mean_term
    )
    mixed_out = forward_tokens[0].astype(jnp.float32) + fwd_sum.total()
    section_input = passed_along(mixed_out.astype(jnp.bfloat16)[None], "section", 1)
    section_gradient = passed_along(token_grad.astype(jnp.bfloat16)[None], "section", -1)
    return (section_input, section_gradient)


def solution(mesh):
    rows = P("section", "expert", None)
    weights = P("section", "expert", None, None)
    return jax.shard_map(
        per_device,
        mesh=mesh,
        in_specs=(rows,) * 7 + (P("section", None),) + (weights,) * 3,
        out_specs=(rows, rows),
        check_vma=False,
    )
```

```python
import functools

import jax
import jax.numpy as jnp
from jax import lax
from jax.experimental import pallas as pl
from jax.experimental.pallas import tpu as pltpu
from jax.sharding import PartitionSpec as P

norm_epsilon = 1e-06
CORES = 2
LANES = 128
TILE = 256
ROWS_AT_ONCE = 256
MIB = 1 << 20
IN_HBM = pl.BlockSpec(memory_space=pl.ANY)
IN_VMEM = pl.BlockSpec(memory_space=pltpu.VMEM)
IN_SMEM = pl.BlockSpec(memory_space=pltpu.SMEM)


def ring_order(chips):
    return [*range(0, chips, 2), *reversed(range(1, chips, 2))]


def ring_route(devices, distance):
    order = ring_order(devices // CORES)
    chips = len(order)
    return [
        (chip * CORES + core, order[(place + distance) % chips] * CORES + core)
        for place, chip in enumerate(order)
        for core in range(CORES)
    ]


def core_route(devices):
    return [(i, i ^ 1) for i in range(devices)]


def passed_along(block, axis, distance):
    size = lax.axis_size(axis)
    return lax.ppermute(block, axis, [(i, (i + distance) % size) for i in range(size)])


def after(arrays, others):
    count = len(arrays)
    return lax.optimization_barrier((*arrays, *others))[:count]


class RingGather:
    def __init__(self, block):
        self.blocks = [block]
        self.newest = (block, block)
        self.left = lax.axis_size("expert") // CORES // 2

    def step(self, others=()):
        devices = lax.axis_size("expert")
        behind, ahead = after(self.newest, others)
        self.left -= 1
        if not self.left:
            half = behind.shape[0] // 2
            behind, ahead = behind[:half], ahead[half:]
        behind = lax.ppermute(behind, "expert", ring_route(devices, 1))
        ahead = lax.ppermute(ahead, "expert", ring_route(devices, -1))
        self.newest = (behind, ahead)
        self.blocks += self.newest


class RingScatter:
    def __init__(self, parts):
        self.parts = parts
        self.newest = ()
        self.reach = self.left = lax.axis_size("expert") // CORES // 2

    def step(self, others=()):
        devices = lax.axis_size("expert")
        to_behind, to_ahead = self.parts[2 * self.left - 1], self.parts[2 * self.left]
        if self.left == self.reach:
            behind, ahead = to_behind, to_ahead
        else:
            behind, ahead = after(self.newest, others)
            half = self.parts[0].shape[0] // 2
            if self.left == self.reach - 1:
                behind = jnp.concatenate([added(to_behind[:half], behind), to_behind[half:]])
                ahead = jnp.concatenate([to_ahead[:half], added(to_ahead[half:], ahead)])
            else:
                behind, ahead = added(to_behind, behind), added(to_ahead, ahead)
        self.left -= 1
        behind = lax.ppermute(behind, "expert", ring_route(devices, -1))
        ahead = lax.ppermute(ahead, "expert", ring_route(devices, 1))
        self.newest = (behind, ahead)

    def total(self):
        behind, ahead = self.newest
        return self.parts[0].astype(jnp.float32) + behind.astype(jnp.float32) + ahead.astype(jnp.float32)


def added(left, right):
    return (left.astype(jnp.float32) + right.astype(jnp.float32)).astype(jnp.bfloat16)


def inverse_norm(rows):
    return lax.rsqrt(jnp.mean(rows * rows, axis=-1, keepdims=True) + norm_epsilon)


def normalize(tokens, gain_row):
    tokens_f32 = tokens.astype(jnp.float32)
    return (tokens_f32 * inverse_norm(tokens_f32) * gain_row).astype(jnp.bfloat16)


def payload_body(devices, *refs):
    sources, out, held, arrived = refs[:8], refs[8], refs[9:16], refs[16]
    width = sources[0].shape[1]
    places = [*held, out.at[:, pl.ds(2 * width, width)]]
    copies = [
        pltpu.make_async_copy(source, place, arrived.at[i])
        for i, (source, place) in enumerate(zip(sources, places))
    ]
    for copy in copies:
        copy.start()
    for copy in copies:
        copy.wait()
    rows, gain, routing = held[:2], held[2], (held[3:5], held[5:7])
    for i, tokens in enumerate(rows):
        out[:, i * width : (i + 1) * width] = normalize(tokens[...], gain[...])
    shape = (out.shape[1] - 3 * width, out.shape[0])
    row = lax.broadcasted_iota(jnp.int32, shape, 0)
    part, expert = lax.div(row, devices), lax.rem(row, devices)
    table = jnp.zeros(shape, jnp.float32)
    for batch, (choices, gates) in enumerate(routing):
        for i in range(choices.shape[0]):
            named = (expert == choices[i : i + 1, :]) & (lax.div(part, 2) == batch)
            table += jnp.where(named, gates[i : i + 1, :], 0.0)
    high = table.astype(jnp.bfloat16).astype(jnp.float32)
    table = jnp.where(lax.rem(part, 2) == 0, high, table - high)
    out[:, 3 * width :] = table.T.astype(jnp.bfloat16)


def payload(forward, backward, cotangent, gain, forward_routing, backward_routing, devices):
    rows, width = forward.shape
    table = -(-4 * devices // LANES) * LANES
    sources = (forward, backward, gain, *forward_routing, *backward_routing, cotangent)
    return pl.pallas_call(
        functools.partial(payload_body, devices),
        in_specs=[IN_HBM] * 8,
        out_specs=IN_VMEM,
        out_shape=jax.ShapeDtypeStruct((rows, 3 * width + table), jnp.bfloat16),
        scratch_shapes=[pltpu.VMEM(source.shape, source.dtype) for source in sources[:7]]
        + [pltpu.SemaphoreType.DMA((8,))],
        compiler_params=pltpu.CompilerParams(vmem_limit_bytes=60 * MIB),
        cost_estimate=pl.CostEstimate(flops=1, bytes_accessed=1, transcendentals=0),
    )(*sources)


def dot_plain(left, right):
    return jnp.dot(left, right, preferred_element_type=jnp.float32)


def dot_trans(left, right):
    return lax.dot_general(
        left, right, (((1,), (1,)), ((), ())), preferred_element_type=jnp.float32
    )


def weights_body(*refs):
    weights, (gate_up, down, done) = refs[:6], refs[6:]
    hidden = weights[0].shape[1]
    copies = []
    for core in range(CORES):
        gate_w, up_w, down_w = weights[3 * core : 3 * core + 3]
        first = gate_up.at[:, pl.ds(2 * core * hidden, hidden)]
        second = gate_up.at[:, pl.ds((2 * core + 1) * hidden, hidden)]
        copies += [(gate_w, first), (up_w, second), (down_w, down.at[pl.ds(core * hidden, hidden)])]
    copies = [pltpu.make_async_copy(*pair, done.at[i]) for i, pair in enumerate(copies)]
    for copy in copies:
        copy.start()
    for copy in copies:
        copy.wait()


def weights_in_vmem(mine, theirs):
    width, hidden = mine[0].shape
    return pl.pallas_call(
        weights_body,
        in_specs=[IN_HBM] * 6,
        out_specs=(IN_VMEM, IN_VMEM),
        out_shape=(
            pltpu.VMEM((width, 2 * CORES * hidden), jnp.bfloat16),
            pltpu.VMEM((CORES * hidden, width), jnp.bfloat16),
        ),
        scratch_shapes=[pltpu.SemaphoreType.DMA((6,))],
        compiler_params=pltpu.CompilerParams(vmem_limit_bytes=38 * MIB),
    )(*mine, *theirs)


def collect(blocks, column, rows, arrived):
    copies, first = [], 0
    for i, block in enumerate(blocks):
        to = rows.at[pl.ds(first, block.shape[0])]
        part = block.at[:, pl.ds(column, rows.shape[1])]
        copies.append(pltpu.make_async_copy(part, to, arrived.at[i]))
        first += block.shape[0]
    for copy in copies:
        copy.start()
    for copy in copies:
        copy.wait()


def backward_body(count, devices, *refs):
    blocks = refs[:count]
    experts, gate_up, down, out, forward_gates, rows, grads, arrived = refs[count:]
    width, hidden = gate_up.shape[0], down.shape[0] // CORES
    collect(blocks, width, rows, arrived)
    table = rows[:, 2 * width :].astype(jnp.float32)
    lane = lax.broadcasted_iota(jnp.int32, table.shape, 1)

    def gate(first, core):
        ours = first * devices + experts[core]
        named = (lane == ours) | (lane == ours + devices)
        return jnp.sum(jnp.where(named, table, 0.0), axis=1, keepdims=True)

    out_lane = lax.broadcasted_iota(jnp.int32, forward_gates.shape, 1)
    forward_gates[...] = jnp.where(out_lane == 0, gate(0, 0), gate(0, 1))
    for core in range(CORES):
        scale = gate(2, core)
        for tile in range(0, hidden, TILE):
            gate_at = pl.ds(2 * core * hidden + tile, TILE)
            up_at = pl.ds((2 * core + 1) * hidden + tile, TILE)
            down_at = pl.ds(core * hidden + tile, TILE)
            gate_act = dot_plain(rows[:, :width], gate_up[:, gate_at])
            up_act = dot_plain(rows[:, :width], gate_up[:, up_at])
            hidden_grad = dot_trans(rows[:, width : 2 * width], down[down_at, :]) * scale
            sigmoid_val = jax.nn.sigmoid(gate_act)
            silu_slope = sigmoid_val * (1.0 + gate_act * (1.0 - sigmoid_val))
            grads[:, gate_at] = (hidden_grad * up_act * silu_slope).astype(jnp.bfloat16)
            grads[:, up_at] = (hidden_grad * (gate_act * sigmoid_val)).astype(jnp.bfloat16)
    for tile in range(0, width, TILE):
        at = pl.ds(tile, TILE)
        out[:, at] = dot_trans(grads[...], gate_up[at, :]).astype(jnp.bfloat16)


def experts_backward(blocks, experts, gate_up, down, devices):
    width = gate_up.shape[0]
    count, rows = sum(b.shape[0] for b in blocks), blocks[0].shape[1] - width
    return pl.pallas_call(
        functools.partial(backward_body, len(blocks), devices),
        in_specs=[IN_HBM] * len(blocks) + [IN_SMEM, IN_VMEM, IN_VMEM],
        out_specs=(IN_VMEM, IN_VMEM),
        out_shape=(
            jax.ShapeDtypeStruct((count, width), jnp.bfloat16),
            jax.ShapeDtypeStruct((count, LANES), jnp.float32),
        ),
        scratch_shapes=[
            pltpu.VMEM((count, rows), jnp.bfloat16),
            pltpu.VMEM((count, gate_up.shape[1]), jnp.bfloat16),
            pltpu.SemaphoreType.DMA((len(blocks),)),
        ],
        compiler_params=pltpu.CompilerParams(vmem_limit_bytes=14 * MIB),
        cost_estimate=pl.CostEstimate(
            flops=1,
            bytes_accessed=1,
            transcendentals=0,
        ),
    )(*blocks, experts, gate_up, down)


def forward_body(count, *refs):
    blocks = refs[:count]
    gates, gate_up, down, out, rows, acts, arrived = refs[count:]
    width, hidden = gate_up.shape[0], down.shape[0] // CORES
    collect(blocks, 0, rows, arrived)
    for core in range(CORES):
        scale = gates[:, core : core + 1]
        for tile in range(0, hidden, TILE):
            gate_at = pl.ds(2 * core * hidden + tile, TILE)
            up_at = pl.ds((2 * core + 1) * hidden + tile, TILE)
            gate_act = dot_plain(rows[...], gate_up[:, gate_at])
            up_act = dot_plain(rows[...], gate_up[:, up_at])
            act = gate_act * jax.nn.sigmoid(gate_act) * up_act * scale
            acts[:, pl.ds(core * hidden + tile, TILE)] = act.astype(jnp.bfloat16)
    for tile in range(0, width, TILE):
        at = pl.ds(tile, TILE)
        out[:, at] = dot_plain(acts[...], down[:, at]).astype(jnp.bfloat16)


def experts_forward(blocks, gates, gate_up, down):
    count, width = sum(b.shape[0] for b in blocks), gate_up.shape[0]
    return pl.pallas_call(
        functools.partial(forward_body, len(blocks)),
        in_specs=[IN_HBM] * len(blocks) + [IN_VMEM, IN_VMEM, IN_VMEM],
        out_specs=IN_VMEM,
        out_shape=jax.ShapeDtypeStruct((count, width), jnp.bfloat16),
        scratch_shapes=[
            pltpu.VMEM((count, width), jnp.bfloat16),
            pltpu.VMEM((count, down.shape[0]), jnp.bfloat16),
            pltpu.SemaphoreType.DMA((len(blocks),)),
        ],
        compiler_params=pltpu.CompilerParams(vmem_limit_bytes=14 * MIB),
        cost_estimate=pl.CostEstimate(
            flops=1,
            bytes_accessed=1,
            transcendentals=0,
        ),
    )(*blocks, gates, gate_up, down)


def grouped(blocks):
    groups, rows = [[]], 0
    for block in blocks:
        if groups[-1] and rows + block.shape[0] > ROWS_AT_ONCE:
            groups.append([])
            rows = 0
        groups[-1].append(block)
        rows += block.shape[0]
    return groups


def ungrouped(outs, groups):
    parts = []
    for out, group in zip(outs, groups):
        first = 0
        for block in group:
            parts.append(out[first : first + block.shape[0]])
            first += block.shape[0]
    return parts


def per_device(
    forward_tokens,
    forward_choice,
    forward_gates,
    backward_tokens,
    backward_cotangent,
    backward_choice,
    backward_gates,
    norm_gain,
    gate_weight,
    up_weight,
    down_weight,
):
    devices = lax.axis_size("expert")
    gain_row = norm_gain[0]
    cotangent = backward_cotangent[0]
    tokens = RingGather(
        payload(
            forward_tokens[0],
            backward_tokens[0],
            cotangent,
            norm_gain,
            (forward_choice[0].T, forward_gates[0].T),
            (backward_choice[0].T, backward_gates[0].T),
            devices,
        )
    )
    mine = (gate_weight[0, 0], up_weight[0, 0], down_weight[0, 0])
    me = lax.axis_index("expert").astype(jnp.int32)
    experts = jnp.stack([me, me + 1 - 2 * lax.rem(me, 2)])

    tokens.step()
    theirs = after(mine, tokens.newest)
    theirs = tuple(lax.ppermute(w, "expert", core_route(devices)) for w in theirs)
    while tokens.left > 1:
        tokens.step()
    early = grouped(tokens.blocks)[:-1]
    theirs = after(theirs, early[-1][-1:])
    gate_up, down = weights_in_vmem(mine, theirs)

    def run_back(blocks):
        return experts_backward(blocks, experts, gate_up, down, devices)

    def run_fwd(blocks, gates):
        return experts_forward(blocks, gates, gate_up, down)

    back_outs = [run_back(group) for group in early]
    tokens.step([out for out, _ in back_outs])
    fwd_outs = [run_fwd(group, gates) for group, (_, gates) in zip(early, back_outs)]
    groups = grouped(tokens.blocks)
    back_outs.append(run_back(after(groups[-1], fwd_outs)))
    back_sum = RingScatter(ungrouped([out for out, _ in back_outs], groups))
    back_sum.step()
    fwd_outs.append(run_fwd(groups[-1], back_outs[-1][1]))
    fwd_sum = RingScatter(ungrouped(fwd_outs, groups))
    back_sum.step()
    fwd_sum.step()
    while back_sum.left:
        arrived = back_sum.newest
        back_sum.step(fwd_sum.newest)
        fwd_sum.step(arrived)
    while fwd_sum.left:
        fwd_sum.step()

    back_f32 = backward_tokens[0].astype(jnp.float32)
    back_inverse = inverse_norm(back_f32)
    scaled = gain_row * back_sum.total()
    mean_term = jnp.mean(back_f32 * scaled, axis=-1, keepdims=True)
    token_grad = (
        cotangent.astype(jnp.float32)
        + back_inverse * scaled
        - back_f32 * back_inverse * back_inverse * back_inverse * mean_term
    )
    mixed_out = forward_tokens[0].astype(jnp.float32) + fwd_sum.total()
    section_input = passed_along(mixed_out.astype(jnp.bfloat16)[None], "section", 1)
    section_gradient = passed_along(token_grad.astype(jnp.bfloat16)[None], "section", -1)
    return (section_input, section_gradient)


def solution(mesh):
    rows = P("section", "expert", None)
    weights = P("section", "expert", None, None)
    return jax.shard_map(
        per_device,
        mesh=mesh,
        in_specs=(rows,) * 7 + (P("section", None),) + (weights,) * 3,
        out_specs=(rows, rows),
        check_vma=False,
    )
```

```python
import functools

import jax
import jax.numpy as jnp
from jax import lax
from jax.experimental import pallas as pl
from jax.experimental.pallas import tpu as pltpu
from jax.sharding import PartitionSpec as P

norm_epsilon = 1e-06
CORES = 2
LANES = 128
TILE = 256
ROWS_AT_ONCE = 256
MIB = 1 << 20
COST = 1
PAUSE = 10**11
IN_HBM = pl.BlockSpec(memory_space=pl.ANY)
IN_VMEM = pl.BlockSpec(memory_space=pltpu.VMEM)
IN_SMEM = pl.BlockSpec(memory_space=pltpu.SMEM)


def ring_order(chips):
    return [*range(0, chips, 2), *reversed(range(1, chips, 2))]


def ring_route(devices, distance):
    order = ring_order(devices // CORES)
    chips = len(order)
    return [
        (chip * CORES + core, order[(place + distance) % chips] * CORES + core)
        for place, chip in enumerate(order)
        for core in range(CORES)
    ]


def core_route(devices):
    return [(i, i ^ 1) for i in range(devices)]


def passed_along(block, axis, distance):
    size = lax.axis_size(axis)
    return lax.ppermute(block, axis, [(i, (i + distance) % size) for i in range(size)])


def joined(*groups):
    return lax.optimization_barrier(groups)


class RingGather:
    def __init__(self, block):
        self.blocks = [block]
        self.newest = (block, block)
        self.left = lax.axis_size("expert") // CORES // 2

    def step(self):
        self.newest = self.moved(*self.newest)
        self.blocks += self.newest
        self.left -= 1

    def last_step(self, first, last):
        behind, ahead = self.newest
        half = behind.shape[0] // 2
        return self.moved(behind[:half, first:last], ahead[half:, first:last])

    def moved(self, behind, ahead):
        devices = lax.axis_size("expert")
        behind = lax.ppermute(behind, "expert", ring_route(devices, 1))
        ahead = lax.ppermute(ahead, "expert", ring_route(devices, -1))
        return behind, ahead


class RingScatter:
    def __init__(self, parts):
        self.parts = parts
        self.newest = ()
        self.reach = self.left = lax.axis_size("expert") // CORES // 2

    def step(self):
        devices = lax.axis_size("expert")
        to_behind, to_ahead = self.parts[2 * self.left - 1], self.parts[2 * self.left]
        if self.left == self.reach:
            behind, ahead = to_behind, to_ahead
        else:
            behind, ahead = self.newest
            half = self.parts[0].shape[0] // 2
            if self.left == self.reach - 1:
                behind = jnp.concatenate([added(to_behind[:half], behind), to_behind[half:]])
                ahead = jnp.concatenate([to_ahead[:half], added(to_ahead[half:], ahead)])
            else:
                behind, ahead = added(to_behind, behind), added(to_ahead, ahead)
        self.left -= 1
        behind = lax.ppermute(behind, "expert", ring_route(devices, -1))
        ahead = lax.ppermute(ahead, "expert", ring_route(devices, 1))
        self.newest = (behind, ahead)

    def total(self):
        behind, ahead = self.newest
        return self.parts[0].astype(jnp.float32) + behind.astype(jnp.float32) + ahead.astype(jnp.float32)


def added(left, right):
    return (left.astype(jnp.float32) + right.astype(jnp.float32)).astype(jnp.bfloat16)


def inverse_norm(rows):
    return lax.rsqrt(jnp.mean(rows * rows, axis=-1, keepdims=True) + norm_epsilon)


def normalize(tokens, gain_row):
    tokens_f32 = tokens.astype(jnp.float32)
    return (tokens_f32 * inverse_norm(tokens_f32) * gain_row).astype(jnp.bfloat16)


def payload_body(devices, *refs):
    sources, out, held, arrived = refs[:8], refs[8], refs[9:16], refs[16]
    width = sources[0].shape[1]
    table_width = out.shape[1] - 3 * width
    first = width + table_width
    places = [*held, out.at[:, pl.ds(first + width, width)]]
    copies = [
        pltpu.make_async_copy(source, place, arrived.at[i])
        for i, (source, place) in enumerate(zip(sources, places))
    ]
    for copy in copies:
        copy.start()
    for copy in copies:
        copy.wait()
    rows, gain, routing = held[:2], held[2], (held[3:5], held[5:7])
    out[:, :width] = normalize(rows[0][...], gain[...])
    out[:, first : first + width] = normalize(rows[1][...], gain[...])
    shape = (table_width, out.shape[0])
    row = lax.broadcasted_iota(jnp.int32, shape, 0)
    part, expert = lax.div(row, devices), lax.rem(row, devices)
    table = jnp.zeros(shape, jnp.float32)
    for batch, (choices, gates) in enumerate(routing):
        for i in range(choices.shape[0]):
            named = (expert == choices[i : i + 1, :]) & (lax.div(part, 2) == batch)
            table += jnp.where(named, gates[i : i + 1, :], 0.0)
    high = table.astype(jnp.bfloat16).astype(jnp.float32)
    table = jnp.where(lax.rem(part, 2) == 0, high, table - high)
    out[:, width:first] = table.T.astype(jnp.bfloat16)


def payload(forward, backward, cotangent, gain, forward_routing, backward_routing, devices):
    rows, width = forward.shape
    table = -(-4 * devices // LANES) * LANES
    sources = (forward, backward, gain, *forward_routing, *backward_routing, cotangent)
    return pl.pallas_call(
        functools.partial(payload_body, devices),
        in_specs=[IN_HBM] * 8,
        out_specs=IN_VMEM,
        out_shape=jax.ShapeDtypeStruct((rows, 3 * width + table), jnp.bfloat16),
        scratch_shapes=[pltpu.VMEM(source.shape, source.dtype) for source in sources[:7]]
        + [pltpu.SemaphoreType.DMA((8,))],
        compiler_params=pltpu.CompilerParams(vmem_limit_bytes=60 * MIB),
        cost_estimate=pl.CostEstimate(flops=1, bytes_accessed=1, transcendentals=0),
    )(*sources)


def dot_plain(left, right):
    return jnp.dot(left, right, preferred_element_type=jnp.float32)


def dot_trans(left, right):
    return lax.dot_general(
        left, right, (((1,), (1,)), ((), ())), preferred_element_type=jnp.float32
    )


def weights_body(*refs):
    weights, (gate_up, down, done) = refs[:6], refs[6:]
    hidden = weights[0].shape[1]
    copies = []
    for core in range(CORES):
        gate_w, up_w, down_w = weights[3 * core : 3 * core + 3]
        first = gate_up.at[:, pl.ds(2 * core * hidden, hidden)]
        second = gate_up.at[:, pl.ds((2 * core + 1) * hidden, hidden)]
        copies += [(gate_w, first), (up_w, second), (down_w, down.at[pl.ds(core * hidden, hidden)])]
    copies = [pltpu.make_async_copy(*pair, done.at[i]) for i, pair in enumerate(copies)]
    for copy in copies:
        copy.start()
    for copy in copies:
        copy.wait()


def weights_in_vmem(mine, theirs):
    width, hidden = mine[0].shape
    return pl.pallas_call(
        weights_body,
        in_specs=[IN_HBM] * 6,
        out_specs=(IN_VMEM, IN_VMEM),
        out_shape=(
            pltpu.VMEM((width, 2 * CORES * hidden), jnp.bfloat16),
            pltpu.VMEM((CORES * hidden, width), jnp.bfloat16),
        ),
        scratch_shapes=[pltpu.SemaphoreType.DMA((6,))],
        compiler_params=pltpu.CompilerParams(vmem_limit_bytes=38 * MIB),
    )(*mine, *theirs)


def collect(blocks, rows, arrived):
    copies, first, columns = [], 0, rows.shape[1]
    for i, block in enumerate(blocks):
        to = rows.at[pl.ds(first, block.shape[0])]
        part = block.at[:, pl.ds(block.shape[1] - columns, columns)]
        copies.append(pltpu.make_async_copy(part, to, arrived.at[i]))
        first += block.shape[0]
    for copy in copies:
        copy.start()
    for copy in copies:
        copy.wait()


def gate_of(table, devices, experts, part, core):
    lane = lax.broadcasted_iota(jnp.int32, table.shape, 1)
    ours = part * devices + experts[core]
    named = (lane == ours) | (lane == ours + devices)
    return jnp.sum(jnp.where(named, table, 0.0), axis=1, keepdims=True)


def grads_body(count, devices, *refs):
    blocks = refs[:count]
    experts, gate_up, down, grads, rows, arrived = refs[count:]
    width, hidden = gate_up.shape[0], down.shape[0] // CORES
    first = rows.shape[1] - 2 * width
    collect(blocks, rows, arrived)
    table = rows[:, :first].astype(jnp.float32)
    normed, cotangent = rows.at[:, pl.ds(first, width)], rows.at[:, pl.ds(first + width, width)]
    for core in range(CORES):
        scale = gate_of(table, devices, experts, 2, core)
        for tile in range(0, hidden, TILE):
            gate_at = pl.ds(2 * core * hidden + tile, TILE)
            up_at = pl.ds((2 * core + 1) * hidden + tile, TILE)
            down_at = pl.ds(core * hidden + tile, TILE)
            gate_act = dot_plain(normed[...], gate_up[:, gate_at])
            up_act = dot_plain(normed[...], gate_up[:, up_at])
            hidden_grad = dot_trans(cotangent[...], down[down_at, :]) * scale
            sigmoid_val = jax.nn.sigmoid(gate_act)
            silu_slope = sigmoid_val * (1.0 + gate_act * (1.0 - sigmoid_val))
            grads[:, gate_at] = (hidden_grad * up_act * silu_slope).astype(jnp.bfloat16)
            grads[:, up_at] = (hidden_grad * (gate_act * sigmoid_val)).astype(jnp.bfloat16)


def hidden_grads(blocks, experts, gate_up, down, devices, table):
    count, width = sum(b.shape[0] for b in blocks), gate_up.shape[0]
    return pl.pallas_call(
        functools.partial(grads_body, len(blocks), devices),
        in_specs=[IN_HBM] * len(blocks) + [IN_SMEM, IN_VMEM, IN_VMEM],
        out_specs=IN_VMEM,
        out_shape=jax.ShapeDtypeStruct((count, gate_up.shape[1]), jnp.bfloat16),
        scratch_shapes=[
            pltpu.VMEM((count, table + 2 * width), jnp.bfloat16),
            pltpu.SemaphoreType.DMA((len(blocks),)),
        ],
        compiler_params=pltpu.CompilerParams(vmem_limit_bytes=14 * MIB),
        cost_estimate=pl.CostEstimate(flops=COST, bytes_accessed=1, transcendentals=0),
    )(*blocks, experts, gate_up, down)


def token_grads_body(grads, gate_up, out):
    for tile in range(0, out.shape[1], TILE):
        at = pl.ds(tile, TILE)
        out[:, at] = dot_trans(grads[...], gate_up[at, :]).astype(jnp.bfloat16)


def token_grads(grads, gate_up, cost=COST):
    return pl.pallas_call(
        token_grads_body,
        in_specs=[IN_VMEM, IN_VMEM],
        out_specs=IN_VMEM,
        out_shape=jax.ShapeDtypeStruct((grads.shape[0], gate_up.shape[0]), jnp.bfloat16),
        compiler_params=pltpu.CompilerParams(vmem_limit_bytes=14 * MIB),
        cost_estimate=pl.CostEstimate(flops=cost, bytes_accessed=1, transcendentals=0),
    )(grads, gate_up)


def forward_body(count, devices, *refs):
    blocks = refs[:count]
    experts, gate_up, down, out, rows, acts, arrived = refs[count:]
    width, hidden = gate_up.shape[0], down.shape[0] // CORES
    collect([block.at[:, pl.ds(0, rows.shape[1])] for block in blocks], rows, arrived)
    table = rows[:, width:].astype(jnp.float32)
    for core in range(CORES):
        scale = gate_of(table, devices, experts, 0, core)
        for tile in range(0, hidden, TILE):
            gate_at = pl.ds(2 * core * hidden + tile, TILE)
            up_at = pl.ds((2 * core + 1) * hidden + tile, TILE)
            gate_act = dot_plain(rows[:, :width], gate_up[:, gate_at])
            up_act = dot_plain(rows[:, :width], gate_up[:, up_at])
            act = gate_act * jax.nn.sigmoid(gate_act) * up_act * scale
            acts[:, pl.ds(core * hidden + tile, TILE)] = act.astype(jnp.bfloat16)
    for tile in range(0, width, TILE):
        at = pl.ds(tile, TILE)
        out[:, at] = dot_plain(acts[...], down[:, at]).astype(jnp.bfloat16)


def experts_forward(blocks, experts, gate_up, down, devices, table):
    count, width = sum(b.shape[0] for b in blocks), gate_up.shape[0]
    return pl.pallas_call(
        functools.partial(forward_body, len(blocks), devices),
        in_specs=[IN_HBM] * len(blocks) + [IN_SMEM, IN_VMEM, IN_VMEM],
        out_specs=IN_VMEM,
        out_shape=jax.ShapeDtypeStruct((count, width), jnp.bfloat16),
        scratch_shapes=[
            pltpu.VMEM((count, width + table), jnp.bfloat16),
            pltpu.VMEM((count, down.shape[0]), jnp.bfloat16),
            pltpu.SemaphoreType.DMA((len(blocks),)),
        ],
        compiler_params=pltpu.CompilerParams(vmem_limit_bytes=14 * MIB),
        cost_estimate=pl.CostEstimate(flops=COST, bytes_accessed=1, transcendentals=0),
    )(*blocks, experts, gate_up, down)


def grouped(blocks):
    groups, rows = [[]], 0
    for block in blocks:
        if groups[-1] and rows + block.shape[0] > ROWS_AT_ONCE:
            groups.append([])
            rows = 0
        groups[-1].append(block)
        rows += block.shape[0]
    return groups


def ungrouped(outs, groups):
    parts = []
    for out, group in zip(outs, groups):
        first = 0
        for block in group:
            parts.append(out[first : first + block.shape[0]])
            first += block.shape[0]
    return parts


def per_device(
    forward_tokens,
    forward_choice,
    forward_gates,
    backward_tokens,
    backward_cotangent,
    backward_choice,
    backward_gates,
    norm_gain,
    gate_weight,
    up_weight,
    down_weight,
):
    devices = lax.axis_size("expert")
    gain_row = norm_gain[0]
    cotangent = backward_cotangent[0]
    me = lax.axis_index("expert").astype(jnp.int32)
    experts = jnp.stack([me, me + 1 - 2 * lax.rem(me, 2)])
    own = payload(
        forward_tokens[0],
        backward_tokens[0],
        cotangent,
        norm_gain,
        (forward_choice[0].T, forward_gates[0].T),
        (backward_choice[0].T, backward_gates[0].T),
        devices,
    )
    width, columns = forward_tokens.shape[2], own.shape[1]
    table = columns - 3 * width
    tokens = RingGather(own)
    tokens.step()
    mine = (gate_weight[0, 0], up_weight[0, 0], down_weight[0, 0])
    theirs = tuple(lax.ppermute(w, "expert", core_route(devices)) for w in mine)

    def run_back(blocks):
        return hidden_grads(blocks, experts, gate_up, down, devices, table)

    def run_fwd(blocks):
        return experts_forward(blocks, experts, gate_up, down, devices, table)

    while tokens.left > 3:
        tokens.step()
    tokens.newest, theirs = joined(tokens.newest, theirs)
    fwd_groups = grouped(tokens.blocks)
    tokens.step()
    gate_up, down = weights_in_vmem(mine, theirs)
    fwd_outs = [run_fwd(group) for group in fwd_groups]
    tokens.newest, fwd_outs[-1] = joined(tokens.newest, fwd_outs[-1])
    back_groups = grouped(tokens.blocks)[:-1]
    fwd_groups.append(tokens.blocks[-2:])
    tokens.step()
    back_outs = [token_grads(run_back(group), gate_up) for group in back_groups]
    fwd_outs.append(run_fwd(fwd_groups[-1]))
    tokens.newest, fwd_outs[-1], back_outs[-1] = joined(
        tokens.newest, fwd_outs[-1], back_outs[-1]
    )
    fwd_last = tokens.last_step(0, width + table)
    back_last = tokens.last_step(width, columns)
    fwd_groups.append([*tokens.blocks[-2:], *fwd_last])
    fwd_outs.append(run_fwd(fwd_groups[-1]))
    fwd_sum = RingScatter(ungrouped(fwd_outs, fwd_groups))
    fwd_sum.step()
    for group in grouped([*tokens.blocks, *back_last])[len(back_groups) :]:
        fwd_outs[-1], group[0] = joined(fwd_outs[-1], group[0])
        grads = run_back(group)
        if fwd_sum.left == fwd_sum.reach - 1:
            fwd_sum.newest, grads = joined(fwd_sum.newest, grads)
            fwd_sum.step()
        back_groups.append(group)
        back_outs.append(token_grads(grads, gate_up, PAUSE))
    back_sum = RingScatter(ungrouped(back_outs, back_groups))
    while back_sum.left:
        back_sum.step()
        if fwd_sum.left:
            fwd_sum.step()

    back_f32 = backward_tokens[0].astype(jnp.float32)
    back_inverse = inverse_norm(back_f32)
    scaled = gain_row * back_sum.total()
    mean_term = jnp.mean(back_f32 * scaled, axis=-1, keepdims=True)
    token_grad = (
        cotangent.astype(jnp.float32)
        + back_inverse * scaled
        - back_f32 * back_inverse * back_inverse * back_inverse * mean_term
    )
    mixed_out = forward_tokens[0].astype(jnp.float32) + fwd_sum.total()
    section_input = passed_along(mixed_out.astype(jnp.bfloat16)[None], "section", 1)
    section_gradient = passed_along(token_grad.astype(jnp.bfloat16)[None], "section", -1)
    return (section_input, section_gradient)


def solution(mesh):
    rows = P("section", "expert", None)
    weights = P("section", "expert", None, None)
    return jax.shard_map(
        per_device,
        mesh=mesh,
        in_specs=(rows,) * 7 + (P("section", None),) + (weights,) * 3,
        out_specs=(rows, rows),
        check_vma=False,
    )
```

```python
import functools

import jax
import jax.numpy as jnp
from jax import lax
from jax.experimental import pallas as pl
from jax.experimental.pallas import tpu as pltpu
from jax.sharding import PartitionSpec as P

norm_epsilon = 1e-06
CORES = 2
LANES = 128
TILE = 256
ROWS_AT_ONCE = 256
MIB = 1 << 20
COST = 1
IN_TURN = 2
PAUSE = 10**11
IN_HBM = pl.BlockSpec(memory_space=pl.ANY)
IN_VMEM = pl.BlockSpec(memory_space=pltpu.VMEM)
IN_SMEM = pl.BlockSpec(memory_space=pltpu.SMEM)


def ring_order(chips):
    return [*range(0, chips, 2), *reversed(range(1, chips, 2))]


def ring_route(devices, distance):
    order = ring_order(devices // CORES)
    chips = len(order)
    return [
        (chip * CORES + core, order[(place + distance) % chips] * CORES + core)
        for place, chip in enumerate(order)
        for core in range(CORES)
    ]


def core_route(devices):
    return [(i, i ^ 1) for i in range(devices)]


def passed_along(block, axis, distance):
    size = lax.axis_size(axis)
    return lax.ppermute(block, axis, [(i, (i + distance) % size) for i in range(size)])


def joined(*groups):
    return lax.optimization_barrier(groups)


class RingGather:
    def __init__(self, block):
        self.blocks = [block]
        self.newest = (block, block)
        self.left = lax.axis_size("expert") // CORES // 2

    def step(self):
        self.newest = self.moved(*self.newest)
        self.blocks += self.newest
        self.left -= 1

    def last_step(self, first, last):
        behind, ahead = self.newest
        half = behind.shape[0] // 2
        return self.moved(behind[:half, first:last], ahead[half:, first:last])

    def moved(self, behind, ahead):
        devices = lax.axis_size("expert")
        behind = lax.ppermute(behind, "expert", ring_route(devices, 1))
        ahead = lax.ppermute(ahead, "expert", ring_route(devices, -1))
        return behind, ahead


class RingScatter:
    def __init__(self, parts):
        self.parts = parts
        self.newest = ()
        self.reach = self.left = lax.axis_size("expert") // CORES // 2

    def step(self):
        devices = lax.axis_size("expert")
        to_behind, to_ahead = self.parts[2 * self.left - 1], self.parts[2 * self.left]
        if self.left == self.reach:
            behind, ahead = to_behind, to_ahead
        else:
            behind, ahead = self.newest
            half = self.parts[0].shape[0] // 2
            if self.left == self.reach - 1:
                behind = jnp.concatenate([added(to_behind[:half], behind), to_behind[half:]])
                ahead = jnp.concatenate([to_ahead[:half], added(to_ahead[half:], ahead)])
            else:
                behind, ahead = added(to_behind, behind), added(to_ahead, ahead)
        self.left -= 1
        behind = lax.ppermute(behind, "expert", ring_route(devices, -1))
        ahead = lax.ppermute(ahead, "expert", ring_route(devices, 1))
        self.newest = (behind, ahead)

    def total(self):
        behind, ahead = self.newest
        return self.parts[0].astype(jnp.float32) + behind.astype(jnp.float32) + ahead.astype(jnp.float32)


def added(left, right):
    return (left.astype(jnp.float32) + right.astype(jnp.float32)).astype(jnp.bfloat16)


def inverse_norm(rows):
    return lax.rsqrt(jnp.mean(rows * rows, axis=-1, keepdims=True) + norm_epsilon)


def normalize(tokens, gain_row):
    tokens_f32 = tokens.astype(jnp.float32)
    return (tokens_f32 * inverse_norm(tokens_f32) * gain_row).astype(jnp.bfloat16)


def payload_body(devices, *refs):
    sources, out, held, arrived = refs[:8], refs[8], refs[9:16], refs[16]
    width = sources[0].shape[1]
    table_width = out.shape[1] - 3 * width
    first = width + table_width
    places = [*held, out.at[:, pl.ds(first + width, width)]]
    copies = [
        pltpu.make_async_copy(source, place, arrived.at[i])
        for i, (source, place) in enumerate(zip(sources, places))
    ]
    first_core = lax.rem(lax.axis_index("expert"), CORES) == 0
    for at_once, core in ((len(copies), jnp.logical_not(first_core)), (IN_TURN, first_core)):

        @pl.when(core)
        def _():
            for first in range(0, len(copies), at_once):
                for copy in copies[first : first + at_once]:
                    copy.start()
                for copy in copies[first : first + at_once]:
                    copy.wait()

    rows, gain, routing = held[:2], held[2], (held[3:5], held[5:7])
    out[:, :width] = normalize(rows[0][...], gain[...])
    out[:, first : first + width] = normalize(rows[1][...], gain[...])
    shape = (table_width, out.shape[0])
    row = lax.broadcasted_iota(jnp.int32, shape, 0)
    part, expert = lax.div(row, devices), lax.rem(row, devices)
    table = jnp.zeros(shape, jnp.float32)
    for batch, (choices, gates) in enumerate(routing):
        for i in range(choices.shape[0]):
            named = (expert == choices[i : i + 1, :]) & (lax.div(part, 2) == batch)
            table += jnp.where(named, gates[i : i + 1, :], 0.0)
    high = table.astype(jnp.bfloat16).astype(jnp.float32)
    table = jnp.where(lax.rem(part, 2) == 0, high, table - high)
    out[:, width:first] = table.T.astype(jnp.bfloat16)


def payload(forward, backward, cotangent, gain, forward_routing, backward_routing, devices):
    rows, width = forward.shape
    table = -(-4 * devices // LANES) * LANES
    sources = (forward, backward, gain, *forward_routing, *backward_routing, cotangent)
    return pl.pallas_call(
        functools.partial(payload_body, devices),
        in_specs=[IN_HBM] * 8,
        out_specs=IN_VMEM,
        out_shape=jax.ShapeDtypeStruct((rows, 3 * width + table), jnp.bfloat16),
        scratch_shapes=[pltpu.VMEM(source.shape, source.dtype) for source in sources[:7]]
        + [pltpu.SemaphoreType.DMA((8,))],
        compiler_params=pltpu.CompilerParams(vmem_limit_bytes=60 * MIB),
        cost_estimate=pl.CostEstimate(flops=1, bytes_accessed=1, transcendentals=0),
    )(*sources)


def dot_plain(left, right):
    return jnp.dot(left, right, preferred_element_type=jnp.float32)


def dot_trans(left, right):
    return lax.dot_general(
        left, right, (((1,), (1,)), ((), ())), preferred_element_type=jnp.float32
    )


def weights_body(*refs):
    weights, (gate_up, down, done) = refs[:6], refs[6:]
    hidden = weights[0].shape[1]
    copies = []
    for core in range(CORES):
        gate_w, up_w, down_w = weights[3 * core : 3 * core + 3]
        first = gate_up.at[:, pl.ds(2 * core * hidden, hidden)]
        second = gate_up.at[:, pl.ds((2 * core + 1) * hidden, hidden)]
        copies += [(gate_w, first), (up_w, second), (down_w, down.at[pl.ds(core * hidden, hidden)])]
    copies = [pltpu.make_async_copy(*pair, done.at[i]) for i, pair in enumerate(copies)]
    for copy in copies:
        copy.start()
    for copy in copies:
        copy.wait()


def weights_in_vmem(mine, theirs):
    width, hidden = mine[0].shape
    return pl.pallas_call(
        weights_body,
        in_specs=[IN_HBM] * 6,
        out_specs=(IN_VMEM, IN_VMEM),
        out_shape=(
            pltpu.VMEM((width, 2 * CORES * hidden), jnp.bfloat16),
            pltpu.VMEM((CORES * hidden, width), jnp.bfloat16),
        ),
        scratch_shapes=[pltpu.SemaphoreType.DMA((6,))],
        compiler_params=pltpu.CompilerParams(vmem_limit_bytes=38 * MIB),
    )(*mine, *theirs)


def collect(blocks, rows, arrived):
    copies, first, columns = [], 0, rows.shape[1]
    for i, block in enumerate(blocks):
        to = rows.at[pl.ds(first, block.shape[0])]
        part = block.at[:, pl.ds(block.shape[1] - columns, columns)]
        copies.append(pltpu.make_async_copy(part, to, arrived.at[i]))
        first += block.shape[0]
    for copy in copies:
        copy.start()
    for copy in copies:
        copy.wait()


def gate_of(table, devices, experts, part, core):
    lane = lax.broadcasted_iota(jnp.int32, table.shape, 1)
    ours = part * devices + experts[core]
    named = (lane == ours) | (lane == ours + devices)
    return jnp.sum(jnp.where(named, table, 0.0), axis=1, keepdims=True)


def grads_body(count, devices, *refs):
    blocks = refs[:count]
    experts, gate_up, down, grads, rows, arrived = refs[count:]
    width, hidden = gate_up.shape[0], down.shape[0] // CORES
    first = rows.shape[1] - 2 * width
    collect(blocks, rows, arrived)
    table = rows[:, :first].astype(jnp.float32)
    normed, cotangent = rows.at[:, pl.ds(first, width)], rows.at[:, pl.ds(first + width, width)]
    for core in range(CORES):
        scale = gate_of(table, devices, experts, 2, core)
        for tile in range(0, hidden, TILE):
            gate_at = pl.ds(2 * core * hidden + tile, TILE)
            up_at = pl.ds((2 * core + 1) * hidden + tile, TILE)
            down_at = pl.ds(core * hidden + tile, TILE)
            gate_act = dot_plain(normed[...], gate_up[:, gate_at])
            up_act = dot_plain(normed[...], gate_up[:, up_at])
            hidden_grad = dot_trans(cotangent[...], down[down_at, :]) * scale
            sigmoid_val = jax.nn.sigmoid(gate_act)
            silu_slope = sigmoid_val * (1.0 + gate_act * (1.0 - sigmoid_val))
            grads[:, gate_at] = (hidden_grad * up_act * silu_slope).astype(jnp.bfloat16)
            grads[:, up_at] = (hidden_grad * (gate_act * sigmoid_val)).astype(jnp.bfloat16)


def hidden_grads(blocks, experts, gate_up, down, devices, table):
    count, width = sum(b.shape[0] for b in blocks), gate_up.shape[0]
    return pl.pallas_call(
        functools.partial(grads_body, len(blocks), devices),
        in_specs=[IN_HBM] * len(blocks) + [IN_SMEM, IN_VMEM, IN_VMEM],
        out_specs=IN_VMEM,
        out_shape=jax.ShapeDtypeStruct((count, gate_up.shape[1]), jnp.bfloat16),
        scratch_shapes=[
            pltpu.VMEM((count, table + 2 * width), jnp.bfloat16),
            pltpu.SemaphoreType.DMA((len(blocks),)),
        ],
        compiler_params=pltpu.CompilerParams(vmem_limit_bytes=14 * MIB),
        cost_estimate=pl.CostEstimate(flops=COST, bytes_accessed=1, transcendentals=0),
    )(*blocks, experts, gate_up, down)


def token_grads_body(grads, gate_up, out):
    for tile in range(0, out.shape[1], TILE):
        at = pl.ds(tile, TILE)
        out[:, at] = dot_trans(grads[...], gate_up[at, :]).astype(jnp.bfloat16)


def token_grads(grads, gate_up, cost=COST):
    return pl.pallas_call(
        token_grads_body,
        in_specs=[IN_VMEM, IN_VMEM],
        out_specs=IN_VMEM,
        out_shape=jax.ShapeDtypeStruct((grads.shape[0], gate_up.shape[0]), jnp.bfloat16),
        compiler_params=pltpu.CompilerParams(vmem_limit_bytes=14 * MIB),
        cost_estimate=pl.CostEstimate(flops=cost, bytes_accessed=1, transcendentals=0),
    )(grads, gate_up)


def forward_body(count, devices, *refs):
    blocks = refs[:count]
    experts, gate_up, down, out, rows, acts, arrived = refs[count:]
    width, hidden = gate_up.shape[0], down.shape[0] // CORES
    collect([block.at[:, pl.ds(0, rows.shape[1])] for block in blocks], rows, arrived)
    table = rows[:, width:].astype(jnp.float32)
    for core in range(CORES):
        scale = gate_of(table, devices, experts, 0, core)
        for tile in range(0, hidden, TILE):
            gate_at = pl.ds(2 * core * hidden + tile, TILE)
            up_at = pl.ds((2 * core + 1) * hidden + tile, TILE)
            gate_act = dot_plain(rows[:, :width], gate_up[:, gate_at])
            up_act = dot_plain(rows[:, :width], gate_up[:, up_at])
            act = gate_act * jax.nn.sigmoid(gate_act) * up_act * scale
            acts[:, pl.ds(core * hidden + tile, TILE)] = act.astype(jnp.bfloat16)
    for tile in range(0, width, TILE):
        at = pl.ds(tile, TILE)
        out[:, at] = dot_plain(acts[...], down[:, at]).astype(jnp.bfloat16)


def experts_forward(blocks, experts, gate_up, down, devices, table):
    count, width = sum(b.shape[0] for b in blocks), gate_up.shape[0]
    return pl.pallas_call(
        functools.partial(forward_body, len(blocks), devices),
        in_specs=[IN_HBM] * len(blocks) + [IN_SMEM, IN_VMEM, IN_VMEM],
        out_specs=IN_VMEM,
        out_shape=jax.ShapeDtypeStruct((count, width), jnp.bfloat16),
        scratch_shapes=[
            pltpu.VMEM((count, width + table), jnp.bfloat16),
            pltpu.VMEM((count, down.shape[0]), jnp.bfloat16),
            pltpu.SemaphoreType.DMA((len(blocks),)),
        ],
        compiler_params=pltpu.CompilerParams(vmem_limit_bytes=14 * MIB),
        cost_estimate=pl.CostEstimate(flops=COST, bytes_accessed=1, transcendentals=0),
    )(*blocks, experts, gate_up, down)


def grouped(blocks):
    groups, rows = [[]], 0
    for block in blocks:
        if groups[-1] and rows + block.shape[0] > ROWS_AT_ONCE:
            groups.append([])
            rows = 0
        groups[-1].append(block)
        rows += block.shape[0]
    return groups


def ungrouped(outs, groups):
    parts = []
    for out, group in zip(outs, groups):
        first = 0
        for block in group:
            parts.append(out[first : first + block.shape[0]])
            first += block.shape[0]
    return parts


def copied_body(array, copy, done):
    step = pltpu.make_async_copy(array, copy, done)
    step.start()
    step.wait()


def copied(array):
    return pl.pallas_call(
        copied_body,
        in_specs=[IN_HBM],
        out_specs=IN_HBM,
        out_shape=jax.ShapeDtypeStruct(array.shape, array.dtype),
        scratch_shapes=[pltpu.SemaphoreType.DMA],
        compiler_params=pltpu.CompilerParams(vmem_limit_bytes=MIB),
        cost_estimate=pl.CostEstimate(flops=PAUSE, bytes_accessed=1, transcendentals=0),
    )(array)


def per_device(
    forward_tokens,
    forward_choice,
    forward_gates,
    backward_tokens,
    backward_cotangent,
    backward_choice,
    backward_gates,
    norm_gain,
    gate_weight,
    up_weight,
    down_weight,
):
    devices = lax.axis_size("expert")
    gain_row = norm_gain[0]
    cotangent = backward_cotangent[0]
    me = lax.axis_index("expert").astype(jnp.int32)
    experts = jnp.stack([me, me + 1 - 2 * lax.rem(me, 2)])
    own = payload(
        forward_tokens[0],
        backward_tokens[0],
        cotangent,
        norm_gain,
        (forward_choice[0].T, forward_gates[0].T),
        (backward_choice[0].T, backward_gates[0].T),
        devices,
    )
    width, columns = forward_tokens.shape[2], own.shape[1]
    table = columns - 3 * width
    tokens = RingGather(own)
    tokens.step()
    mine = (gate_weight[0, 0], up_weight[0, 0], down_weight[0, 0])
    theirs = tuple(lax.ppermute(w, "expert", core_route(devices)) for w in mine)

    def run_back(blocks):
        return hidden_grads(blocks, experts, gate_up, down, devices, table)

    def run_fwd(blocks):
        return experts_forward(blocks, experts, gate_up, down, devices, table)

    while tokens.left > 3:
        tokens.step()
    tokens.newest, theirs = joined(tokens.newest, theirs)
    fwd_groups = grouped(tokens.blocks)
    tokens.step()
    gate_up, down = weights_in_vmem(mine, theirs)
    fwd_outs = [run_fwd(group) for group in fwd_groups]
    tokens.newest, fwd_outs[-1] = joined(tokens.newest, fwd_outs[-1])
    back_groups = grouped(tokens.blocks)[:-1]
    fwd_groups.append(tokens.blocks[-2:])
    tokens.step()
    back_outs = [token_grads(run_back(group), gate_up) for group in back_groups]
    fwd_outs.append(run_fwd(fwd_groups[-1]))
    tokens.newest, fwd_outs[-1], back_outs[-1] = joined(
        tokens.newest, fwd_outs[-1], back_outs[-1]
    )
    fwd_last = tokens.last_step(0, width + table)
    back_last = tokens.last_step(width, columns)
    fwd_groups.append([*tokens.blocks[-2:], *fwd_last])
    fwd_outs.append(run_fwd(fwd_groups[-1]))
    fwd_sum = RingScatter(ungrouped(fwd_outs, fwd_groups))
    fwd_sum.step()
    for group in grouped([*tokens.blocks, *back_last])[len(back_groups) :]:
        fwd_outs[-1], group[0] = joined(fwd_outs[-1], group[0])
        grads = run_back(group)
        if fwd_sum.left == fwd_sum.reach - 1:
            fwd_sum.newest, grads = joined(fwd_sum.newest, grads)
            fwd_sum.step()
        back_groups.append(group)
        back_outs.append(token_grads(grads, gate_up, PAUSE))
    back_sum = RingScatter(ungrouped(back_outs, back_groups))
    while back_sum.left:
        back_sum.step()
        if fwd_sum.left:
            fwd_sum.step()

    back_f32 = backward_tokens[0].astype(jnp.float32)
    back_inverse = inverse_norm(back_f32)
    scaled = gain_row * back_sum.total()
    mean_term = jnp.mean(back_f32 * scaled, axis=-1, keepdims=True)
    token_grad = (
        cotangent.astype(jnp.float32)
        + back_inverse * scaled
        - back_f32 * back_inverse * back_inverse * back_inverse * mean_term
    )
    mixed_out = forward_tokens[0].astype(jnp.float32) + fwd_sum.total()
    section_input = passed_along(mixed_out.astype(jnp.bfloat16)[None], "section", 1)
    section_gradient = passed_along(token_grad.astype(jnp.bfloat16)[None], "section", -1)
    return (copied(section_input), section_gradient)


def solution(mesh):
    rows = P("section", "expert", None)
    weights = P("section", "expert", None, None)
    return jax.shard_map(
        per_device,
        mesh=mesh,
        in_specs=(rows,) * 7 + (P("section", None),) + (weights,) * 3,
        out_specs=(rows, rows),
        check_vma=False,
    )
```

```python
import functools

import jax
import jax.numpy as jnp
from jax import lax
from jax.experimental import pallas as pl
from jax.experimental.pallas import tpu as pltpu
from jax.sharding import PartitionSpec as P

norm_epsilon = 1e-06
CORES = 2
LANES = 128
TILE = 256
ROWS_AT_ONCE = 256
MIB = 1 << 20
COST = 1
IN_TURN = 2
PAUSE = 10**11
IN_HBM = pl.BlockSpec(memory_space=pl.ANY)
IN_VMEM = pl.BlockSpec(memory_space=pltpu.VMEM)
IN_SMEM = pl.BlockSpec(memory_space=pltpu.SMEM)


def ring_order(chips):
    return [*range(0, chips, 2), *reversed(range(1, chips, 2))]


def ring_route(devices, distance):
    order = ring_order(devices // CORES)
    chips = len(order)
    return [
        (chip * CORES + core, order[(place + distance) % chips] * CORES + core)
        for place, chip in enumerate(order)
        for core in range(CORES)
    ]


def core_route(devices):
    return [(i, i ^ 1) for i in range(devices)]


def passed_along(block, axis, distance):
    size = lax.axis_size(axis)
    return lax.ppermute(block, axis, [(i, (i + distance) % size) for i in range(size)])


def joined(*groups):
    return lax.optimization_barrier(groups)


class RingGather:
    def __init__(self, block):
        self.blocks = [block]
        self.newest = (block, block)
        self.left = lax.axis_size("expert") // CORES // 2

    def step(self):
        self.newest = self.moved(*self.newest)
        self.blocks += self.newest
        self.left -= 1

    def last_step(self, first, last):
        behind, ahead = self.newest
        half = behind.shape[0] // 2
        return self.moved(behind[:half, first:last], ahead[half:, first:last])

    def moved(self, behind, ahead):
        devices = lax.axis_size("expert")
        behind = lax.ppermute(behind, "expert", ring_route(devices, 1))
        ahead = lax.ppermute(ahead, "expert", ring_route(devices, -1))
        return behind, ahead


class RingScatter:
    def __init__(self, parts):
        self.parts = parts
        self.newest = ()
        self.reach = self.left = lax.axis_size("expert") // CORES // 2

    def step(self):
        devices = lax.axis_size("expert")
        to_behind, to_ahead = self.parts[2 * self.left - 1], self.parts[2 * self.left]
        if self.left == self.reach:
            behind, ahead = to_behind, to_ahead
        else:
            behind, ahead = self.newest
            half = self.parts[0].shape[0] // 2
            if self.left == self.reach - 1:
                behind = jnp.concatenate([added(to_behind[:half], behind), to_behind[half:]])
                ahead = jnp.concatenate([to_ahead[:half], added(to_ahead[half:], ahead)])
            else:
                behind, ahead = added(to_behind, behind), added(to_ahead, ahead)
        self.left -= 1
        behind = lax.ppermute(behind, "expert", ring_route(devices, -1))
        ahead = lax.ppermute(ahead, "expert", ring_route(devices, 1))
        self.newest = (behind, ahead)

    def total(self):
        behind, ahead = self.newest
        return self.parts[0].astype(jnp.float32) + behind.astype(jnp.float32) + ahead.astype(jnp.float32)


def added(left, right):
    return (left.astype(jnp.float32) + right.astype(jnp.float32)).astype(jnp.bfloat16)


def inverse_norm(rows):
    return lax.rsqrt(jnp.mean(rows * rows, axis=-1, keepdims=True) + norm_epsilon)


def normalize(tokens, gain_row):
    tokens_f32 = tokens.astype(jnp.float32)
    return (tokens_f32 * inverse_norm(tokens_f32) * gain_row).astype(jnp.bfloat16)


def payload_body(devices, *refs):
    sources, out, held, arrived = refs[:8], refs[8], refs[9:16], refs[16]
    width = sources[0].shape[1]
    table_width = out.shape[1] - 3 * width
    first = width + table_width
    places = [*held, out.at[:, pl.ds(first + width, width)]]
    copies = [
        pltpu.make_async_copy(source, place, arrived.at[i])
        for i, (source, place) in enumerate(zip(sources, places))
    ]
    first_core = lax.rem(lax.axis_index("expert"), CORES) == 0
    other_core = jnp.logical_not(first_core)

    @pl.when(first_core)
    def _():
        for first in range(0, len(copies), IN_TURN):
            for copy in copies[first : first + IN_TURN]:
                copy.start()
            for copy in copies[first : first + IN_TURN]:
                copy.wait()

    @pl.when(other_core)
    def _():
        for copy in copies:
            copy.start()

    def needed(some):
        @pl.when(other_core)
        def _():
            for copy in some:
                copy.wait()

    needed(copies[2:7])
    rows, gain, routing = held[:2], held[2], (held[3:5], held[5:7])
    shape = (table_width, out.shape[0])
    row = lax.broadcasted_iota(jnp.int32, shape, 0)
    part, expert = lax.div(row, devices), lax.rem(row, devices)
    table = jnp.zeros(shape, jnp.float32)
    for batch, (choices, gates) in enumerate(routing):
        for i in range(choices.shape[0]):
            named = (expert == choices[i : i + 1, :]) & (lax.div(part, 2) == batch)
            table += jnp.where(named, gates[i : i + 1, :], 0.0)
    high = table.astype(jnp.bfloat16).astype(jnp.float32)
    table = jnp.where(lax.rem(part, 2) == 0, high, table - high)
    out[:, width:first] = table.T.astype(jnp.bfloat16)
    needed(copies[:1])
    out[:, :width] = normalize(rows[0][...], gain[...])
    needed(copies[1:2])
    out[:, first : first + width] = normalize(rows[1][...], gain[...])
    needed(copies[7:])


def payload(forward, backward, cotangent, gain, forward_routing, backward_routing, devices):
    rows, width = forward.shape
    table = -(-4 * devices // LANES) * LANES
    sources = (forward, backward, gain, *forward_routing, *backward_routing, cotangent)
    return pl.pallas_call(
        functools.partial(payload_body, devices),
        in_specs=[IN_HBM] * 8,
        out_specs=IN_VMEM,
        out_shape=jax.ShapeDtypeStruct((rows, 3 * width + table), jnp.bfloat16),
        scratch_shapes=[pltpu.VMEM(source.shape, source.dtype) for source in sources[:7]]
        + [pltpu.SemaphoreType.DMA((8,))],
        compiler_params=pltpu.CompilerParams(vmem_limit_bytes=60 * MIB),
        cost_estimate=pl.CostEstimate(flops=1, bytes_accessed=1, transcendentals=0),
    )(*sources)


def dot_plain(left, right):
    return jnp.dot(left, right, preferred_element_type=jnp.float32)


def dot_trans(left, right):
    return lax.dot_general(
        left, right, (((1,), (1,)), ((), ())), preferred_element_type=jnp.float32
    )


def weights_body(*refs):
    weights, (gate_up, down, done) = refs[:6], refs[6:]
    hidden = weights[0].shape[1]
    copies = []
    for core in range(CORES):
        gate_w, up_w, down_w = weights[3 * core : 3 * core + 3]
        first = gate_up.at[:, pl.ds(2 * core * hidden, hidden)]
        second = gate_up.at[:, pl.ds((2 * core + 1) * hidden, hidden)]
        copies += [(gate_w, first), (up_w, second), (down_w, down.at[pl.ds(core * hidden, hidden)])]
    copies = [pltpu.make_async_copy(*pair, done.at[i]) for i, pair in enumerate(copies)]
    for copy in copies:
        copy.start()
    for copy in copies:
        copy.wait()


def weights_in_vmem(mine, theirs):
    width, hidden = mine[0].shape
    return pl.pallas_call(
        weights_body,
        in_specs=[IN_HBM] * 6,
        out_specs=(IN_VMEM, IN_VMEM),
        out_shape=(
            pltpu.VMEM((width, 2 * CORES * hidden), jnp.bfloat16),
            pltpu.VMEM((CORES * hidden, width), jnp.bfloat16),
        ),
        scratch_shapes=[pltpu.SemaphoreType.DMA((6,))],
        compiler_params=pltpu.CompilerParams(vmem_limit_bytes=38 * MIB),
    )(*mine, *theirs)


def collect(blocks, rows, arrived):
    copies, first, columns = [], 0, rows.shape[1]
    for i, block in enumerate(blocks):
        to = rows.at[pl.ds(first, block.shape[0])]
        part = block.at[:, pl.ds(block.shape[1] - columns, columns)]
        copies.append(pltpu.make_async_copy(part, to, arrived.at[i]))
        first += block.shape[0]
    for copy in copies:
        copy.start()
    for copy in copies:
        copy.wait()


def gate_of(table, devices, experts, part, core):
    lane = lax.broadcasted_iota(jnp.int32, table.shape, 1)
    ours = part * devices + experts[core]
    named = (lane == ours) | (lane == ours + devices)
    return jnp.sum(jnp.where(named, table, 0.0), axis=1, keepdims=True)


def grads_body(count, devices, *refs):
    blocks = refs[:count]
    experts, gate_up, down, grads, rows, arrived = refs[count:]
    width, hidden = gate_up.shape[0], down.shape[0] // CORES
    first = rows.shape[1] - 2 * width
    collect(blocks, rows, arrived)
    table = rows[:, :first].astype(jnp.float32)
    normed, cotangent = rows.at[:, pl.ds(first, width)], rows.at[:, pl.ds(first + width, width)]
    for core in range(CORES):
        scale = gate_of(table, devices, experts, 2, core)
        for tile in range(0, hidden, TILE):
            gate_at = pl.ds(2 * core * hidden + tile, TILE)
            up_at = pl.ds((2 * core + 1) * hidden + tile, TILE)
            down_at = pl.ds(core * hidden + tile, TILE)
            gate_act = dot_plain(normed[...], gate_up[:, gate_at])
            up_act = dot_plain(normed[...], gate_up[:, up_at])
            hidden_grad = dot_trans(cotangent[...], down[down_at, :]) * scale
            sigmoid_val = jax.nn.sigmoid(gate_act)
            silu_slope = sigmoid_val * (1.0 + gate_act * (1.0 - sigmoid_val))
            grads[:, gate_at] = (hidden_grad * up_act * silu_slope).astype(jnp.bfloat16)
            grads[:, up_at] = (hidden_grad * (gate_act * sigmoid_val)).astype(jnp.bfloat16)


def hidden_grads(blocks, experts, gate_up, down, devices, table):
    count, width = sum(b.shape[0] for b in blocks), gate_up.shape[0]
    return pl.pallas_call(
        functools.partial(grads_body, len(blocks), devices),
        in_specs=[IN_HBM] * len(blocks) + [IN_SMEM, IN_VMEM, IN_VMEM],
        out_specs=IN_VMEM,
        out_shape=jax.ShapeDtypeStruct((count, gate_up.shape[1]), jnp.bfloat16),
        scratch_shapes=[
            pltpu.VMEM((count, table + 2 * width), jnp.bfloat16),
            pltpu.SemaphoreType.DMA((len(blocks),)),
        ],
        compiler_params=pltpu.CompilerParams(vmem_limit_bytes=14 * MIB),
        cost_estimate=pl.CostEstimate(flops=COST, bytes_accessed=1, transcendentals=0),
    )(*blocks, experts, gate_up, down)


def token_grads_body(grads, gate_up, out):
    for tile in range(0, out.shape[1], TILE):
        at = pl.ds(tile, TILE)
        out[:, at] = dot_trans(grads[...], gate_up[at, :]).astype(jnp.bfloat16)


def token_grads(grads, gate_up, cost=COST):
    return pl.pallas_call(
        token_grads_body,
        in_specs=[IN_VMEM, IN_VMEM],
        out_specs=IN_VMEM,
        out_shape=jax.ShapeDtypeStruct((grads.shape[0], gate_up.shape[0]), jnp.bfloat16),
        compiler_params=pltpu.CompilerParams(vmem_limit_bytes=14 * MIB),
        cost_estimate=pl.CostEstimate(flops=cost, bytes_accessed=1, transcendentals=0),
    )(grads, gate_up)


def forward_body(count, devices, *refs):
    blocks = refs[:count]
    experts, gate_up, down, out, rows, acts, arrived = refs[count:]
    width, hidden = gate_up.shape[0], down.shape[0] // CORES
    collect([block.at[:, pl.ds(0, rows.shape[1])] for block in blocks], rows, arrived)
    table = rows[:, width:].astype(jnp.float32)
    for core in range(CORES):
        scale = gate_of(table, devices, experts, 0, core)
        for tile in range(0, hidden, TILE):
            gate_at = pl.ds(2 * core * hidden + tile, TILE)
            up_at = pl.ds((2 * core + 1) * hidden + tile, TILE)
            gate_act = dot_plain(rows[:, :width], gate_up[:, gate_at])
            up_act = dot_plain(rows[:, :width], gate_up[:, up_at])
            act = gate_act * jax.nn.sigmoid(gate_act) * up_act * scale
            acts[:, pl.ds(core * hidden + tile, TILE)] = act.astype(jnp.bfloat16)
    for tile in range(0, width, TILE):
        at = pl.ds(tile, TILE)
        out[:, at] = dot_plain(acts[...], down[:, at]).astype(jnp.bfloat16)


def experts_forward(blocks, experts, gate_up, down, devices, table):
    count, width = sum(b.shape[0] for b in blocks), gate_up.shape[0]
    return pl.pallas_call(
        functools.partial(forward_body, len(blocks), devices),
        in_specs=[IN_HBM] * len(blocks) + [IN_SMEM, IN_VMEM, IN_VMEM],
        out_specs=IN_VMEM,
        out_shape=jax.ShapeDtypeStruct((count, width), jnp.bfloat16),
        scratch_shapes=[
            pltpu.VMEM((count, width + table), jnp.bfloat16),
            pltpu.VMEM((count, down.shape[0]), jnp.bfloat16),
            pltpu.SemaphoreType.DMA((len(blocks),)),
        ],
        compiler_params=pltpu.CompilerParams(vmem_limit_bytes=14 * MIB),
        cost_estimate=pl.CostEstimate(flops=COST, bytes_accessed=1, transcendentals=0),
    )(*blocks, experts, gate_up, down)


def grouped(blocks):
    groups, rows = [[]], 0
    for block in blocks:
        if groups[-1] and rows + block.shape[0] > ROWS_AT_ONCE:
            groups.append([])
            rows = 0
        groups[-1].append(block)
        rows += block.shape[0]
    return groups


def ungrouped(outs, groups):
    parts = []
    for out, group in zip(outs, groups):
        first = 0
        for block in group:
            parts.append(out[first : first + block.shape[0]])
            first += block.shape[0]
    return parts


def copied_body(array, copy, done):
    step = pltpu.make_async_copy(array, copy, done)
    step.start()
    step.wait()


def copied(array):
    return pl.pallas_call(
        copied_body,
        in_specs=[IN_HBM],
        out_specs=IN_HBM,
        out_shape=jax.ShapeDtypeStruct(array.shape, array.dtype),
        scratch_shapes=[pltpu.SemaphoreType.DMA],
        compiler_params=pltpu.CompilerParams(vmem_limit_bytes=MIB),
        cost_estimate=pl.CostEstimate(flops=PAUSE, bytes_accessed=1, transcendentals=0),
    )(array)


def per_device(
    forward_tokens,
    forward_choice,
    forward_gates,
    backward_tokens,
    backward_cotangent,
    backward_choice,
    backward_gates,
    norm_gain,
    gate_weight,
    up_weight,
    down_weight,
):
    devices = lax.axis_size("expert")
    gain_row = norm_gain[0]
    cotangent = backward_cotangent[0]
    me = lax.axis_index("expert").astype(jnp.int32)
    experts = jnp.stack([me, me + 1 - 2 * lax.rem(me, 2)])
    own = payload(
        forward_tokens[0],
        backward_tokens[0],
        cotangent,
        norm_gain,
        (forward_choice[0].T, forward_gates[0].T),
        (backward_choice[0].T, backward_gates[0].T),
        devices,
    )
    width, columns = forward_tokens.shape[2], own.shape[1]
    table = columns - 3 * width
    tokens = RingGather(own)
    tokens.step()
    mine = (gate_weight[0, 0], up_weight[0, 0], down_weight[0, 0])
    theirs = tuple(lax.ppermute(w, "expert", core_route(devices)) for w in mine)

    def run_back(blocks):
        return hidden_grads(blocks, experts, gate_up, down, devices, table)

    def run_fwd(blocks):
        return experts_forward(blocks, experts, gate_up, down, devices, table)

    while tokens.left > 3:
        tokens.step()
    tokens.newest, theirs = joined(tokens.newest, theirs)
    fwd_groups = grouped(tokens.blocks)
    tokens.step()
    gate_up, down = weights_in_vmem(mine, theirs)
    fwd_outs = [run_fwd(group) for group in fwd_groups]
    tokens.newest, fwd_outs[-1] = joined(tokens.newest, fwd_outs[-1])
    back_groups = grouped(tokens.blocks)[:-1]
    fwd_groups.append(tokens.blocks[-2:])
    tokens.step()
    back_outs = [token_grads(run_back(group), gate_up) for group in back_groups]
    fwd_outs.append(run_fwd(fwd_groups[-1]))
    tokens.newest, fwd_outs[-1], back_outs[-1] = joined(
        tokens.newest, fwd_outs[-1], back_outs[-1]
    )
    fwd_last = tokens.last_step(0, width + table)
    back_last = tokens.last_step(width, columns)
    fwd_groups.append([*tokens.blocks[-2:], *fwd_last])
    fwd_outs.append(run_fwd(fwd_groups[-1]))
    fwd_sum = RingScatter(ungrouped(fwd_outs, fwd_groups))
    fwd_sum.step()
    for group in grouped([*tokens.blocks, *back_last])[len(back_groups) :]:
        fwd_outs[-1], group[0] = joined(fwd_outs[-1], group[0])
        grads = run_back(group)
        if fwd_sum.left == fwd_sum.reach - 1:
            fwd_sum.newest, grads = joined(fwd_sum.newest, grads)
            fwd_sum.step()
        back_groups.append(group)
        back_outs.append(token_grads(grads, gate_up, PAUSE))
    back_sum = RingScatter(ungrouped(back_outs, back_groups))
    while back_sum.left:
        back_sum.step()
        if fwd_sum.left:
            fwd_sum.step()

    back_f32 = backward_tokens[0].astype(jnp.float32)
    back_inverse = inverse_norm(back_f32)
    scaled = gain_row * back_sum.total()
    mean_term = jnp.mean(back_f32 * scaled, axis=-1, keepdims=True)
    token_grad = (
        cotangent.astype(jnp.float32)
        + back_inverse * scaled
        - back_f32 * back_inverse * back_inverse * back_inverse * mean_term
    )
    mixed_out = forward_tokens[0].astype(jnp.float32) + fwd_sum.total()
    section_input = passed_along(mixed_out.astype(jnp.bfloat16)[None], "section", 1)
    section_gradient = passed_along(token_grad.astype(jnp.bfloat16)[None], "section", -1)
    return (copied(section_input), section_gradient)


def solution(mesh):
    rows = P("section", "expert", None)
    weights = P("section", "expert", None, None)
    return jax.shard_map(
        per_device,
        mesh=mesh,
        in_specs=(rows,) * 7 + (P("section", None),) + (weights,) * 3,
        out_specs=(rows, rows),
        check_vma=False,
    )
```

```python
import functools

import jax
import jax.numpy as jnp
from jax import lax
from jax.experimental import pallas as pl
from jax.experimental.pallas import tpu as pltpu
from jax.sharding import PartitionSpec as P

norm_epsilon = 1e-06
CORES = 2
LANES = 128
TILE = 256
ROWS_AT_ONCE = 256
MIB = 1 << 20
COST = 1
IN_TURN = 2
PAUSE = 10**11
IN_HBM = pl.BlockSpec(memory_space=pl.ANY)
IN_VMEM = pl.BlockSpec(memory_space=pltpu.VMEM)
IN_SMEM = pl.BlockSpec(memory_space=pltpu.SMEM)


def ring_order(chips):
    return [*range(0, chips, 2), *reversed(range(1, chips, 2))]


def ring_route(devices, distance):
    order = ring_order(devices // CORES)
    chips = len(order)
    return [
        (chip * CORES + core, order[(place + distance) % chips] * CORES + core)
        for place, chip in enumerate(order)
        for core in range(CORES)
    ]


def core_route(devices):
    return [(i, i ^ 1) for i in range(devices)]


def passed_along(block, axis, distance):
    size = lax.axis_size(axis)
    return lax.ppermute(block, axis, [(i, (i + distance) % size) for i in range(size)])


def joined(*groups):
    return lax.optimization_barrier(groups)


class RingGather:
    def __init__(self, block):
        self.blocks = [block]
        self.newest = (block, block)
        self.left = lax.axis_size("expert") // CORES // 2

    def step(self):
        self.newest = self.moved(*self.newest)
        self.blocks += self.newest
        self.left -= 1

    def last_step(self, first, last):
        behind, ahead = self.newest
        half = behind.shape[0] // 2
        return self.moved(behind[:half, first:last], ahead[half:, first:last])

    def moved(self, behind, ahead):
        devices = lax.axis_size("expert")
        behind = lax.ppermute(behind, "expert", ring_route(devices, 1))
        ahead = lax.ppermute(ahead, "expert", ring_route(devices, -1))
        return behind, ahead


class RingScatter:
    def __init__(self, parts):
        self.parts = parts
        self.newest = ()
        self.reach = self.left = lax.axis_size("expert") // CORES // 2

    def step(self):
        devices = lax.axis_size("expert")
        to_behind, to_ahead = self.parts[2 * self.left - 1], self.parts[2 * self.left]
        if self.left == self.reach:
            behind, ahead = to_behind, to_ahead
        else:
            behind, ahead = self.newest
            half = self.parts[0].shape[0] // 2
            if self.left == self.reach - 1:
                behind = jnp.concatenate([added(to_behind[:half], behind), to_behind[half:]])
                ahead = jnp.concatenate([to_ahead[:half], added(to_ahead[half:], ahead)])
            else:
                behind, ahead = added(to_behind, behind), added(to_ahead, ahead)
        self.left -= 1
        behind = lax.ppermute(behind, "expert", ring_route(devices, -1))
        ahead = lax.ppermute(ahead, "expert", ring_route(devices, 1))
        self.newest = (behind, ahead)

    def total(self):
        behind, ahead = self.newest
        return self.parts[0].astype(jnp.float32) + behind.astype(jnp.float32) + ahead.astype(jnp.float32)


def added(left, right):
    return (left.astype(jnp.float32) + right.astype(jnp.float32)).astype(jnp.bfloat16)


def inverse_norm(rows):
    return lax.rsqrt(jnp.mean(rows * rows, axis=-1, keepdims=True) + norm_epsilon)


def normalize(tokens, gain_row):
    tokens_f32 = tokens.astype(jnp.float32)
    return (tokens_f32 * inverse_norm(tokens_f32) * gain_row).astype(jnp.bfloat16)


def payload_body(devices, *refs):
    sources, out, held, arrived = refs[:8], refs[8], refs[9:16], refs[16]
    width = sources[0].shape[1]
    table_width = out.shape[1] - 3 * width
    first = width + table_width
    places = [*held, out.at[:, pl.ds(first + width, width)]]
    copies = [
        pltpu.make_async_copy(source, place, arrived.at[i])
        for i, (source, place) in enumerate(zip(sources, places))
    ]
    first_core = lax.rem(lax.axis_index("expert"), CORES) == 0
    other_core = jnp.logical_not(first_core)

    @pl.when(first_core)
    def _():
        for first in range(0, len(copies), IN_TURN):
            for copy in copies[first : first + IN_TURN]:
                copy.start()
            for copy in copies[first : first + IN_TURN]:
                copy.wait()

    @pl.when(other_core)
    def _():
        for copy in copies:
            copy.start()

    def needed(some):
        @pl.when(other_core)
        def _():
            for copy in some:
                copy.wait()

    needed(copies[2:7])
    rows, gain, routing = held[:2], held[2], (held[3:5], held[5:7])
    shape = (table_width, out.shape[0])
    row = lax.broadcasted_iota(jnp.int32, shape, 0)
    part, expert = lax.div(row, devices), lax.rem(row, devices)
    table = jnp.zeros(shape, jnp.float32)
    for batch, (choices, gates) in enumerate(routing):
        for i in range(choices.shape[0]):
            named = (expert == choices[i : i + 1, :]) & (lax.div(part, 2) == batch)
            table += jnp.where(named, gates[i : i + 1, :], 0.0)
    high = table.astype(jnp.bfloat16).astype(jnp.float32)
    table = jnp.where(lax.rem(part, 2) == 0, high, table - high)
    out[:, width:first] = table.T.astype(jnp.bfloat16)
    needed(copies[:1])
    out[:, :width] = normalize(rows[0][...], gain[...])
    needed(copies[1:2])
    out[:, first : first + width] = normalize(rows[1][...], gain[...])
    needed(copies[7:])


def payload(forward, backward, cotangent, gain, forward_routing, backward_routing, devices):
    rows, width = forward.shape
    table = -(-4 * devices // LANES) * LANES
    sources = (forward, backward, gain, *forward_routing, *backward_routing, cotangent)
    return pl.pallas_call(
        functools.partial(payload_body, devices),
        in_specs=[IN_HBM] * 8,
        out_specs=IN_VMEM,
        out_shape=jax.ShapeDtypeStruct((rows, 3 * width + table), jnp.bfloat16),
        scratch_shapes=[pltpu.VMEM(source.shape, source.dtype) for source in sources[:7]]
        + [pltpu.SemaphoreType.DMA((8,))],
        compiler_params=pltpu.CompilerParams(vmem_limit_bytes=60 * MIB),
        cost_estimate=pl.CostEstimate(flops=1, bytes_accessed=1, transcendentals=0),
    )(*sources)


def dot_plain(left, right):
    return jnp.dot(left, right, preferred_element_type=jnp.float32)


def dot_trans(left, right):
    return lax.dot_general(
        left, right, (((1,), (1,)), ((), ())), preferred_element_type=jnp.float32
    )


def weights_body(*refs):
    weights, (gate_up, down, done) = refs[:6], refs[6:]
    hidden = weights[0].shape[1]
    copies = []
    for core in range(CORES):
        gate_w, up_w, down_w = weights[3 * core : 3 * core + 3]
        first = gate_up.at[:, pl.ds(2 * core * hidden, hidden)]
        second = gate_up.at[:, pl.ds((2 * core + 1) * hidden, hidden)]
        copies += [(gate_w, first), (up_w, second), (down_w, down.at[pl.ds(core * hidden, hidden)])]
    copies = [pltpu.make_async_copy(*pair, done.at[i]) for i, pair in enumerate(copies)]
    for copy in copies:
        copy.start()
    for copy in copies:
        copy.wait()


def weights_in_vmem(mine, theirs):
    width, hidden = mine[0].shape
    return pl.pallas_call(
        weights_body,
        in_specs=[IN_HBM] * 6,
        out_specs=(IN_VMEM, IN_VMEM),
        out_shape=(
            pltpu.VMEM((width, 2 * CORES * hidden), jnp.bfloat16),
            pltpu.VMEM((CORES * hidden, width), jnp.bfloat16),
        ),
        scratch_shapes=[pltpu.SemaphoreType.DMA((6,))],
        compiler_params=pltpu.CompilerParams(vmem_limit_bytes=42 * MIB),
    )(*mine, *theirs)


def collect(blocks, rows, arrived):
    copies, first, columns = [], 0, rows.shape[1]
    for i, block in enumerate(blocks):
        to = rows.at[pl.ds(first, block.shape[0])]
        part = block.at[:, pl.ds(block.shape[1] - columns, columns)]
        copies.append(pltpu.make_async_copy(part, to, arrived.at[i]))
        first += block.shape[0]
    for copy in copies:
        copy.start()
    for copy in copies:
        copy.wait()


def gate_of(table, devices, experts, part, core):
    lane = lax.broadcasted_iota(jnp.int32, table.shape, 1)
    ours = part * devices + experts[core]
    named = (lane == ours) | (lane == ours + devices)
    return jnp.sum(jnp.where(named, table, 0.0), axis=1, keepdims=True)


def grads_body(count, devices, *refs):
    blocks = refs[:count]
    experts, gate_up, down, grads, rows, arrived = refs[count:]
    width, hidden = gate_up.shape[0], down.shape[0] // CORES
    first = rows.shape[1] - 2 * width
    collect(blocks, rows, arrived)
    table = rows[:, :first].astype(jnp.float32)
    normed, cotangent = rows.at[:, pl.ds(first, width)], rows.at[:, pl.ds(first + width, width)]
    for core in range(CORES):
        scale = gate_of(table, devices, experts, 2, core)
        for tile in range(0, hidden, TILE):
            gate_at = pl.ds(2 * core * hidden + tile, TILE)
            up_at = pl.ds((2 * core + 1) * hidden + tile, TILE)
            down_at = pl.ds(core * hidden + tile, TILE)
            gate_act = dot_plain(normed[...], gate_up[:, gate_at])
            up_act = dot_plain(normed[...], gate_up[:, up_at])
            hidden_grad = dot_trans(cotangent[...], down[down_at, :]) * scale
            sigmoid_val = jax.nn.sigmoid(gate_act)
            silu_slope = sigmoid_val * (1.0 + gate_act * (1.0 - sigmoid_val))
            grads[:, gate_at] = (hidden_grad * up_act * silu_slope).astype(jnp.bfloat16)
            grads[:, up_at] = (hidden_grad * (gate_act * sigmoid_val)).astype(jnp.bfloat16)


def hidden_grads(blocks, experts, gate_up, down, devices, table):
    count, width = sum(b.shape[0] for b in blocks), gate_up.shape[0]
    return pl.pallas_call(
        functools.partial(grads_body, len(blocks), devices),
        in_specs=[IN_HBM] * len(blocks) + [IN_SMEM, IN_VMEM, IN_VMEM],
        out_specs=IN_VMEM,
        out_shape=jax.ShapeDtypeStruct((count, gate_up.shape[1]), jnp.bfloat16),
        scratch_shapes=[
            pltpu.VMEM((count, table + 2 * width), jnp.bfloat16),
            pltpu.SemaphoreType.DMA((len(blocks),)),
        ],
        compiler_params=pltpu.CompilerParams(vmem_limit_bytes=10 * MIB),
        cost_estimate=pl.CostEstimate(flops=COST, bytes_accessed=1, transcendentals=0),
    )(*blocks, experts, gate_up, down)


def token_grads_body(grads, gate_up, out):
    for tile in range(0, out.shape[1], TILE):
        at = pl.ds(tile, TILE)
        out[:, at] = dot_trans(grads[...], gate_up[at, :]).astype(jnp.bfloat16)


def token_grads(grads, gate_up, cost=COST):
    return pl.pallas_call(
        token_grads_body,
        in_specs=[IN_VMEM, IN_VMEM],
        out_specs=IN_VMEM,
        out_shape=jax.ShapeDtypeStruct((grads.shape[0], gate_up.shape[0]), jnp.bfloat16),
        compiler_params=pltpu.CompilerParams(vmem_limit_bytes=10 * MIB),
        cost_estimate=pl.CostEstimate(flops=cost, bytes_accessed=1, transcendentals=0),
    )(grads, gate_up)


def forward_body(count, devices, *refs):
    blocks = refs[:count]
    experts, gate_up, down, out, rows, acts, arrived = refs[count:]
    width, hidden = gate_up.shape[0], down.shape[0] // CORES
    collect([block.at[:, pl.ds(0, rows.shape[1])] for block in blocks], rows, arrived)
    table = rows[:, width:].astype(jnp.float32)
    for core in range(CORES):
        scale = gate_of(table, devices, experts, 0, core)
        for tile in range(0, hidden, TILE):
            gate_at = pl.ds(2 * core * hidden + tile, TILE)
            up_at = pl.ds((2 * core + 1) * hidden + tile, TILE)
            gate_act = dot_plain(rows[:, :width], gate_up[:, gate_at])
            up_act = dot_plain(rows[:, :width], gate_up[:, up_at])
            act = gate_act * jax.nn.sigmoid(gate_act) * up_act * scale
            acts[:, pl.ds(core * hidden + tile, TILE)] = act.astype(jnp.bfloat16)
    for tile in range(0, width, TILE):
        at = pl.ds(tile, TILE)
        out[:, at] = dot_plain(acts[...], down[:, at]).astype(jnp.bfloat16)


def experts_forward(blocks, experts, gate_up, down, devices, table):
    count, width = sum(b.shape[0] for b in blocks), gate_up.shape[0]
    return pl.pallas_call(
        functools.partial(forward_body, len(blocks), devices),
        in_specs=[IN_HBM] * len(blocks) + [IN_SMEM, IN_VMEM, IN_VMEM],
        out_specs=IN_VMEM,
        out_shape=jax.ShapeDtypeStruct((count, width), jnp.bfloat16),
        scratch_shapes=[
            pltpu.VMEM((count, width + table), jnp.bfloat16),
            pltpu.VMEM((count, down.shape[0]), jnp.bfloat16),
            pltpu.SemaphoreType.DMA((len(blocks),)),
        ],
        compiler_params=pltpu.CompilerParams(vmem_limit_bytes=10 * MIB),
        cost_estimate=pl.CostEstimate(flops=COST, bytes_accessed=1, transcendentals=0),
    )(*blocks, experts, gate_up, down)


def grouped(blocks):
    groups, rows = [[]], 0
    for block in blocks:
        if groups[-1] and rows + block.shape[0] > ROWS_AT_ONCE:
            groups.append([])
            rows = 0
        groups[-1].append(block)
        rows += block.shape[0]
    return groups


def ungrouped(outs, groups):
    parts = []
    for out, group in zip(outs, groups):
        first = 0
        for block in group:
            parts.append(out[first : first + block.shape[0]])
            first += block.shape[0]
    return parts


def copied_body(array, copy, done):
    step = pltpu.make_async_copy(array, copy, done)
    step.start()
    step.wait()


def copied(array):
    return pl.pallas_call(
        copied_body,
        in_specs=[IN_HBM],
        out_specs=IN_HBM,
        out_shape=jax.ShapeDtypeStruct(array.shape, array.dtype),
        scratch_shapes=[pltpu.SemaphoreType.DMA],
        compiler_params=pltpu.CompilerParams(vmem_limit_bytes=MIB),
        cost_estimate=pl.CostEstimate(flops=PAUSE, bytes_accessed=1, transcendentals=0),
    )(array)


def per_device(
    forward_tokens,
    forward_choice,
    forward_gates,
    backward_tokens,
    backward_cotangent,
    backward_choice,
    backward_gates,
    norm_gain,
    gate_weight,
    up_weight,
    down_weight,
):
    devices = lax.axis_size("expert")
    gain_row = norm_gain[0]
    cotangent = backward_cotangent[0]
    me = lax.axis_index("expert").astype(jnp.int32)
    experts = jnp.stack([me, me + 1 - 2 * lax.rem(me, 2)])
    own = payload(
        forward_tokens[0],
        backward_tokens[0],
        cotangent,
        norm_gain,
        (forward_choice[0].T, forward_gates[0].T),
        (backward_choice[0].T, backward_gates[0].T),
        devices,
    )
    width, columns = forward_tokens.shape[2], own.shape[1]
    table = columns - 3 * width
    tokens = RingGather(own)
    tokens.step()
    mine = (gate_weight[0, 0], up_weight[0, 0], down_weight[0, 0])
    theirs = tuple(lax.ppermute(w, "expert", core_route(devices)) for w in mine)

    def run_back(blocks):
        return hidden_grads(blocks, experts, gate_up, down, devices, table)

    def run_fwd(blocks):
        return experts_forward(blocks, experts, gate_up, down, devices, table)

    while tokens.left > 3:
        tokens.step()
    tokens.newest, theirs = joined(tokens.newest, theirs)
    fwd_groups = grouped(tokens.blocks)
    tokens.step()
    gate_up, down = weights_in_vmem(mine, theirs)
    fwd_outs = [run_fwd(group) for group in fwd_groups]
    tokens.newest, fwd_outs[-1] = joined(tokens.newest, fwd_outs[-1])
    back_groups = grouped(tokens.blocks)[:-1]
    fwd_groups.append(tokens.blocks[-2:])
    tokens.step()
    back_outs = [token_grads(run_back(group), gate_up) for group in back_groups]
    fwd_outs.append(run_fwd(fwd_groups[-1]))
    tokens.newest, fwd_outs[-1], back_outs[-1] = joined(
        tokens.newest, fwd_outs[-1], back_outs[-1]
    )
    fwd_last = tokens.last_step(0, width + table)
    back_last = tokens.last_step(width, columns)
    fwd_groups.append([*tokens.blocks[-2:], *fwd_last])
    fwd_outs.append(run_fwd(fwd_groups[-1]))
    fwd_sum = RingScatter(ungrouped(fwd_outs, fwd_groups))
    fwd_sum.step()
    for group in grouped([*tokens.blocks, *back_last])[len(back_groups) :]:
        fwd_outs[-1], group[0] = joined(fwd_outs[-1], group[0])
        grads = run_back(group)
        if fwd_sum.left == fwd_sum.reach - 1:
            fwd_sum.newest, grads = joined(fwd_sum.newest, grads)
            fwd_sum.step()
        back_groups.append(group)
        back_outs.append(token_grads(grads, gate_up, PAUSE))
    back_sum = RingScatter(ungrouped(back_outs, back_groups))
    while back_sum.left:
        back_sum.step()
        if fwd_sum.left:
            fwd_sum.step()

    back_f32 = backward_tokens[0].astype(jnp.float32)
    back_inverse = inverse_norm(back_f32)
    scaled = gain_row * back_sum.total()
    mean_term = jnp.mean(back_f32 * scaled, axis=-1, keepdims=True)
    token_grad = (
        cotangent.astype(jnp.float32)
        + back_inverse * scaled
        - back_f32 * back_inverse * back_inverse * back_inverse * mean_term
    )
    mixed_out = forward_tokens[0].astype(jnp.float32) + fwd_sum.total()
    section_input = passed_along(mixed_out.astype(jnp.bfloat16)[None], "section", 1)
    section_gradient = passed_along(token_grad.astype(jnp.bfloat16)[None], "section", -1)
    return (copied(section_input), section_gradient)


def solution(mesh):
    rows = P("section", "expert", None)
    weights = P("section", "expert", None, None)
    return jax.shard_map(
        per_device,
        mesh=mesh,
        in_specs=(rows,) * 7 + (P("section", None),) + (weights,) * 3,
        out_specs=(rows, rows),
        check_vma=False,
    )
```
